32 devices in a mesh: row: 8 (over z, core), col: 4 (over y, x).
Axes of the slice: x: 2, y: 2, z: 4, core: 2. Of those that a mesh axis runs over, the one named last changes fastest.
Arguments:
- object_field: float32 [2, 2048, 1024], P(None, 'row', 'col'), may hold values from -1.8 to 1.8
- probe: float32 [2, 256, 256], replicated, may hold values from -0.4 to 0.4
- coeffs: float32 [3, 256, 256], replicated, may hold values from 0.5 to 1.5
- patterns: float32 [8, 4, 4, 256, 256], P('row', 'col'), may hold values from 0 to 1
- offsets: int32 [8, 4, 4, 2], P('row', 'col'), may hold values from 0 to 255
Outputs:
- object_out: float32 [2, 2048, 1024], P(None, 'row', 'col')
- coeffs_out: float32 [3, 256, 256], replicated
The draws below stay inside these ranges and needn't reach their ends.
All inputs are finite; a program needn't handle non-finite values.
Results may differ from the reference program's by a relative error of at most 0.0003.
Values sent between devices are 32-bit elements; how exact they have to be, the bound alone decides.
A program may use at most 64 MiB of HBM per device.

```python
import jax
import jax.numpy as jnp
from jax import lax

WIN = 256
TILE = 256
POS = 4
ITERS = 2
NY = 2048
NX = 1024
N_ROW = 8
N_COL = 4


def phased_field(key, rows, cols, low, high):
    amp_key, phase_key = jax.random.split(key)
    amplitude = jax.random.uniform(amp_key, (rows, cols), jnp.float32, low, high)
    phase = jax.random.uniform(phase_key, (rows, cols), jnp.float32, -jnp.pi, jnp.pi)
    return jnp.stack([amplitude * jnp.cos(phase), amplitude * jnp.sin(phase)])


def draw_object_field(key, part):
    folded = jax.random.fold_in(key, 11)
    return phased_field(folded, NY, NX, 0.5, 1.5)


def draw_probe(key, part):
    folded = jax.random.fold_in(key, 23)
    return phased_field(folded, WIN, WIN, 0.15, 0.35)


def set_ends(entries, stream_key, least, largest):
    longest = entries.shape.index(max(entries.shape))
    spots = []
    for shift in (0, 1):
        where = [jax.random.randint(jax.random.fold_in(stream_key, axis), (), 0, length) for axis, length in enumerate(entries.shape)]
        where[longest] = (where[longest] + shift) % entries.shape[longest]
        spots.append(tuple(where))
    return entries.at[spots[0]].set(least).at[spots[1]].set(largest)


def level_of(stream_key, shape, cuts, least, largest):
    level = 1.0
    for axis_at, blocks in cuts:
        steps = jax.random.uniform(jax.random.fold_in(jax.random.fold_in(stream_key, 6), axis_at), (blocks,), jnp.float32, least / len(cuts), largest / len(cuts))
        level = level * jnp.repeat(jnp.exp(steps), shape[axis_at] // blocks).reshape((-1,) + (1,) * (len(shape) - 1 - axis_at))
    return level


def setup_inputs(seed: int = 0) -> dict:
    streams_of = jax.random.split(jax.random.key(seed), 6)
    object_field = draw_object_field(jax.random.fold_in(streams_of[5], 71), 0)
    probe = draw_probe(jax.random.fold_in(streams_of[5], 71), 0)
    coeffs = jnp.clip(jax.random.uniform(streams_of[2], (3, WIN, WIN), jnp.float32, 0.5, 1.5), 0.5, 1.5)
    patterns = jnp.clip(1.0 * jax.random.uniform(streams_of[3], (N_ROW, N_COL, POS, WIN, WIN), jnp.float32) ** level_of(streams_of[3], (N_ROW, N_COL, POS, WIN, WIN), ((0, 8), (1, 4)), -0.2, 0.2), 0.0, 1.0)
    offsets = set_ends(jax.random.randint(streams_of[4], (N_ROW, N_COL, POS, 2), 0, TILE), jax.random.fold_in(streams_of[4], 1), 0, TILE - 1).astype(jnp.int32)
    return dict(object_field=object_field, probe=probe, coeffs=coeffs, patterns=patterns, offsets=offsets)


STEP_RATE = 0.2
RIDGE = 1.0
EPSILON = 1e-06

def dft_parts(order):
    index = jnp.arange(order, dtype=jnp.int32)
    product = index[:, None] * index[None, :] % order
    angle = -2.0 * jnp.pi / order * product.astype(jnp.float32)
    factor = 1.0 / jnp.sqrt(jnp.float32(order))
    return (jnp.cos(angle) * factor, jnp.sin(angle) * factor)

def matmul(left, right):
    return jnp.dot(left, right, precision=lax.Precision.HIGHEST, preferred_element_type=jnp.float32)

def transform(real, imag, mat_real, mat_imag):
    first_real = matmul(mat_real, real) - matmul(mat_imag, imag)
    first_imag = matmul(mat_real, imag) + matmul(mat_imag, real)
    second_real = matmul(first_real, mat_real) - matmul(first_imag, mat_imag)
    second_imag = matmul(first_real, mat_imag) + matmul(first_imag, mat_real)
    return (second_real, second_imag)

def window_step(window, probe, coeffs, pattern, mat_real, mat_imag):
    probe_real, probe_imag = (probe[0], probe[1])
    exit_real = probe_real * window[0] - probe_imag * window[1]
    exit_imag = probe_real * window[1] + probe_imag * window[0]
    wave_real, wave_imag = transform(exit_real, exit_imag, mat_real, mat_imag)
    inten = wave_real * wave_real + wave_imag * wave_imag
    lin, quad, cubic = (coeffs[0], coeffs[1], coeffs[2])
    response = inten * (lin + inten * (quad + inten * cubic))
    error = response - pattern
    slope = lin + inten * (2.0 * quad + 3.0 * cubic * inten)
    weight = 2.0 * error * slope
    back_real, back_imag = transform(weight * wave_real, weight * wave_imag, mat_real, -mat_imag)
    grad_real = probe_real * back_real + probe_imag * back_imag
    grad_imag = probe_real * back_imag - probe_imag * back_real
    squared = inten * inten
    gsums = jnp.stack([error * inten, error * squared, error * squared * inten])
    hsums = jnp.stack([squared, squared * squared, squared * squared * squared])
    return (jnp.stack([grad_real, grad_imag]), gsums, hsums)

def reference(object_field, probe, coeffs, patterns, offsets):
    mat_real, mat_imag = dft_parts(WIN)
    half = WIN // 2
    rows_all = object_field.shape[1]
    cols_all = object_field.shape[2]
    count = N_ROW * N_COL * POS
    flat_pats = patterns.reshape(count, WIN, WIN)
    flat_offs = offsets.reshape(count, 2)
    index = jnp.arange(count, dtype=jnp.int32)
    start_rows = index // (N_COL * POS) * TILE + flat_offs[:, 0]
    start_cols = index // POS % N_COL * TILE + flat_offs[:, 1]
    zero = jnp.zeros((), jnp.int32)
    total = 2.0 * rows_all * cols_all
    for turn in range(ITERS):
        padded = jnp.pad(object_field, ((0, 0), (half, half), (half, half)))

        def visit(carry, item):
            grad_pad, gsums, hsums = carry
            row_start, col_start, pattern = item
            window = lax.dynamic_slice(padded, (zero, row_start, col_start), (2, WIN, WIN))
            grad_win, gterm, hterm = window_step(window, probe, coeffs, pattern, mat_real, mat_imag)
            current = lax.dynamic_slice(grad_pad, (zero, row_start, col_start), (2, WIN, WIN))
            grad_pad = lax.dynamic_update_slice(grad_pad, current + grad_win, (zero, row_start, col_start))
            return ((grad_pad, gsums + gterm, hsums + hterm), None)
        start = (jnp.zeros_like(padded), jnp.zeros((3, WIN, WIN), jnp.float32), jnp.zeros((3, WIN, WIN), jnp.float32))
        (grad_pad, gsums, hsums), _ = lax.scan(visit, start, (start_rows, start_cols, flat_pats))
        grad = grad_pad[:, half:half + rows_all, half:half + cols_all]
        meansq = jnp.sum(grad * grad) / total
        coeffs = coeffs - gsums / (hsums + RIDGE)
        object_field = object_field - STEP_RATE * grad / jnp.sqrt(meansq + EPSILON)
    return (object_field, coeffs)
```

```python
import functools

import jax
import jax.numpy as jnp
import ml_dtypes
import numpy as np
from jax import lax
from jax.experimental import pallas as pl
from jax.experimental.pallas import tpu as pltpu
from jax.sharding import PartitionSpec as P

STEP_RATE = 0.2
RIDGE = 1.0
EPSILON = 1e-06
LANES = 128
CHUNK = 16
F32 = jnp.float32
BF16 = jnp.bfloat16


def dft_halves(order):
    half = order // 2
    index = np.arange(order)
    angle = -2.0 * np.pi / order * (index[:, None] * index[None, :] % order)
    real, imag = np.cos(angle) / np.sqrt(order), np.sin(angle) / np.sqrt(order)
    lefts, rights = [], []
    for parity in (0, 1):
        re, im = real[parity::2, :half], imag[parity::2, :half]
        full = np.block([[re, -im], [im, re]]).astype(np.float32)
        for into, forward in ((lefts, full), (rights, full.T)):
            high = forward.astype(ml_dtypes.bfloat16)
            low = (forward - high.astype(np.float32)).astype(ml_dtypes.bfloat16)
            into.append((high, low))
    wide = lambda pair: np.concatenate([pair[0], pair[0], pair[1]], axis=1)
    tall = lambda pair: np.concatenate([pair[0], pair[0], pair[1]], axis=0)
    on_left = [wide(m) for m in lefts] + [wide(m) for m in rights]
    on_right = [tall(m) for m in rights] + [tall(m) for m in lefts]
    order_of = np.concatenate([index[0::2], index[1::2]])
    perm = (order_of[:, None] == index[None, :]).astype(ml_dtypes.bfloat16)
    on_left.append(np.concatenate([perm] * 3, axis=1))
    on_right.append(np.concatenate([perm.T] * 3, axis=0))
    on_right.append(np.concatenate([perm] * 3, axis=0))
    return jnp.asarray(np.stack(on_left)), jnp.asarray(np.stack(on_right))


def dot(left, right):
    return jnp.dot(left, right, preferred_element_type=F32)


def split(full):
    high = full.astype(BF16)
    return high, (full - high.astype(F32)).astype(BF16)


def split3(full):
    high = full.astype(BF16)
    rest = full - high.astype(F32)
    mid = rest.astype(BF16)
    return high, mid, (rest - mid.astype(F32)).astype(BF16)


def from_left(matrix, full):
    high, low = split(full)
    return dot(matrix, jnp.concatenate([high, low, high], axis=0))


def from_right(full, matrix):
    high, low = split(full)
    return dot(jnp.concatenate([high, low, high], axis=1), matrix)


class Copies:
    def __init__(self, send, recv):
        self.send, self.recv, self.used, self.made = send, recv, 0, []

    def make(self, source, target, row=None, col=None, sends=None, gets=None):
        slot = self.used
        self.used += 1
        where = (lax.axis_index("row") if row is None else row, lax.axis_index("col") if col is None else col)
        copy = pltpu.make_async_remote_copy(
            src_ref=source, dst_ref=target, send_sem=self.send.at[slot], recv_sem=self.recv.at[slot],
            device_id=where, device_id_type=pl.DeviceIdType.MESH,
        )
        made = Copy(copy, sends, gets)
        self.made.append(made)
        return made

    def finish(self):
        for made in self.made:
            made.sent()


def when(condition, act):
    if condition is None:
        act()
    else:
        pl.when(condition)(act)


class Copy:
    def __init__(self, copy, sends, gets):
        self.copy, self.sends, self.gets = copy, sends, gets

    def start(self):
        when(self.sends, self.copy.start)
        return self

    def arrived(self):
        when(self.gets, self.copy.wait_recv)

    def sent(self):
        when(self.sends, self.copy.wait_send)


def both(a, b):
    return b if a is None else a if b is None else a & b


def copies_needed(rows, cols):
    return 128 + 4 * (rows + cols)


def refine_kernel(field_hbm, probe_hbm, coeffs_hbm, pats_hbm, offs, left_hbm, right_hbm,
                  field_out, coeffs_out,
                  ext, grads, gext, pads, psi, phi, highs, lows, probe, coeffs, pats, pats_nat, left, right,
                  stats, half_sums, col_sums, shard, z_sums, new_coeffs,
                  folds, got_x, got_g, relay_in, relay_g, last_x, last_g, relay_last, base, gtile,
                  sq_mine, sq_cols, sq_part, sq_rows, woven,
                  local_sem, send_sem, recv_sem):
    rows, cols = lax.axis_size("row"), lax.axis_size("col")
    r, c = lax.axis_index("row"), lax.axis_index("col")
    depth = rows // 2
    k, z = lax.rem(r, 2), lax.div(r, 2)
    count = pats.shape[0]
    width = probe.shape[1]
    half = width // 2
    size = ext.shape[2]
    tile = size - width
    top = half + tile
    net = Copies(send_sem, recv_sem)

    partner = r + 1 - 2 * k
    beyond = r - 1 + 2 * k
    has_z = (beyond >= 0) & (beyond < rows)
    beyond = lax.rem(beyond + rows, rows)
    odd_c = lax.rem(c, 2)
    step_g = 2 * odd_c - 1
    has_g = (c + step_g >= 0) & (c + step_g < cols)
    has_r = (c - 2 * step_g >= 0) & (c - 2 * step_g < cols)
    col_x = c - step_g
    col_g = lax.rem(c + step_g + cols, cols)
    col_r = lax.rem(c + 2 * step_g + 2 * cols, cols)

    barrier = pltpu.get_barrier_semaphore()
    greeted = 0
    for axis, length, here in (("col", cols, c), ("row", rows, r)):
        for distance in range(1, length):
            other = lax.rem(here + distance, length)
            pl.semaphore_signal(
                barrier, inc=1, device_id=(other, c) if axis == "row" else (r, other),
                device_id_type=pl.DeviceIdType.MESH,
            )
            greeted += 1

    inner = pl.ds(half, tile)
    loads = []

    def load(source, target):
        copy = pltpu.make_async_copy(source, target, local_sem.at[len(loads)])
        copy.start()
        loads.append(copy)
        return copy

    field_loads = [
        load(field_hbm.at[:, :, pl.ds(b * LANES, LANES)], ext.at[:, 1 + b, inner, :]) for b in (0, 1)
    ]
    pats_load = load(pats_hbm.at[0, 0], pats_nat)
    coeffs_load = load(coeffs_hbm, new_coeffs.at[2])
    left_load = load(left_hbm, left)
    right_load = load(right_hbm, right)
    probe_load = load(probe_hbm, probe)

    for edge, b in ((c == 0, 0), (c == cols - 1, 3)):
        @pl.when(edge)
        def _():
            ext[:, b] = jnp.zeros((2, size, LANES), F32)
            gext[:, b] = jnp.zeros((2, size, LANES), F32)
    for edge, start in ((r == 0, 0), (r == rows - 1, top)):
        @pl.when(edge)
        def _():
            ext[:, :, pl.ds(start, half), :] = jnp.zeros((2, 4, half, LANES), F32)
            gext[:, :, pl.ds(start, half), :] = jnp.zeros((2, 4, half, LANES), F32)

    def clear(p, carry):
        for part in (0, 1):
            for b in (0, 4):
                pads[p, part, b] = jnp.zeros((3 * width, LANES), F32)
            for b in (1, 2, 3):
                for start in (0, 2 * width):
                    pads[p, part, b, pl.ds(start, width), :] = jnp.zeros((width, LANES), F32)
        return carry

    lax.fori_loop(0, count, clear, 0)
    for copy in field_loads:
        copy.wait()
    pl.semaphore_wait(barrier, greeted)

    def rows_of(which):
        return half * (1 - k) if which == 0 else half * k

    def side_row(which):
        return top * k if which == 0 else top * (1 - k)

    def edge_row(which):
        return top * (1 - k) if which == 0 else top * k

    def at(start, length):
        return pl.ds(pl.multiple_of(start, 8), length)

    side_dev = (partner, beyond)
    side_has = (None, has_z)

    ends = []
    for which in (1, 0):
        mine = at(half + rows_of(which), half)
        there = at(side_row(which), half)
        ends.append(net.make(ext.at[:, pl.ds(1, 2), mine, :], ext.at[:, pl.ds(1, 2), there, :],
                             row=side_dev[which], sends=side_has[which], gets=side_has[which]).start())

    edge_x, edge_g = 2 - odd_c, 1 + odd_c
    out_x, out_g = 3 * (1 - odd_c), 3 * odd_c
    far_x, far_g = 3 * odd_c, 3 * (1 - odd_c)
    quarter = half // 2
    first_units = [(1, 0), (1, 1), (0, 0), (0, 1)]

    def exchange(units, sources, targets, relays):
        made = {}
        for n, unit in enumerate(units):
            sx, sg1, sg2 = sources(*unit)
            tx, tg1, tg2 = targets(*unit)
            made[unit] = (
                net.make(sx, tx, col=col_x),
                net.make(sg1, tg1, col=col_g, sends=has_g, gets=has_g),
                net.make(sg2, relays.at[n], col=col_r, sends=has_g, gets=has_r),
                net.make(relays.at[n], tg2, col=col_x, sends=has_r, gets=has_g),
            )
        return made

    def push(copies):
        copies[2].start()
        copies[0].start()
        copies[1].start()

    def hand_on(copies):
        copies[2].arrived()
        copies[3].start()

    def first_sources(which, part):
        start = half + rows_of(which)
        return (ext.at[part, edge_x, at(start, half), :],
                ext.at[part, edge_g, at(start, quarter), :],
                ext.at[part, edge_g, at(start + quarter, quarter), :])

    def first_targets(which, part):
        start = half + rows_of(which)
        return (ext.at[part, far_x, at(start, half), :],
                ext.at[part, far_g, at(start, quarter), :],
                ext.at[part, far_g, at(start + quarter, quarter), :])

    side = exchange(first_units, first_sources, first_targets, relay_in)
    for unit in first_units:
        push(side[unit])

    def reorder(full):
        part = dot(jnp.concatenate(split3(full), axis=1), right[4])
        return dot(left[4], jnp.concatenate(split3(part), axis=0))

    pats_load.wait()
    left_load.wait()
    right_load.wait()

    def reorder_pats(p, carry):
        pats[p] = reorder(pats_nat[p])
        return carry

    lax.fori_loop(0, count, reorder_pats, 0)
    hand_on(side[first_units[0]])
    coeffs_load.wait()
    for i in range(3):
        coeffs[i] = reorder(new_coeffs[2, i])
    for unit in first_units[1:]:
        hand_on(side[unit])
    probe_load.wait()

    corners = []
    for which, part in first_units:
        mine = at(half + rows_of(which), half)
        there = at(side_row(which), half)
        for arrivals, b, has in (((0,), out_x, None), ((1, 3), out_g, has_g)):
            for i in arrivals:
                side[(which, part)][i].arrived()
            cond = both(has, side_has[which])
            corners.append(net.make(ext.at[part, b, mine, :], ext.at[part, b, there, :],
                                    row=side_dev[which], sends=cond, gets=cond).start())
    for copy in ends + corners:
        copy.arrived()

    lane = lax.broadcasted_iota(jnp.int32, (1, LANES), 1)

    def place(p):
        oy, ox = offs[0, 0, p, 0], offs[0, 0, p, 1]
        block = lax.div(ox, LANES)
        return oy, block, ox - block * LANES

    def forward(source, into):
        def visit(p, carry):
            oy, block, shift = place(p)
            window = []
            keep = lane < LANES - shift
            for part in (0, 1):
                turned = [
                    pltpu.roll(source[part, block + j, pl.ds(oy, width), :], lax.rem(LANES - shift, LANES), axis=1)
                    for j in range(3)
                ]
                window.append([jnp.where(keep, turned[j], turned[j + 1]) for j in (0, 1)])
            sums, difs = [[], []], [[], []]
            for h in (0, 1):
                pr, pi = probe[0, :, h * LANES:(h + 1) * LANES], probe[1, :, h * LANES:(h + 1) * LANES]
                wr, wi = window[0][h], window[1][h]
                for part, x in ((0, pr * wr - pi * wi), (1, pr * wi + pi * wr)):
                    sums[part].append(x[:half] + x[half:])
                    difs[part].append(x[:half] - x[half:])
            bands = []
            for parity, group in ((0, sums), (1, difs)):
                stack = jnp.concatenate([jnp.concatenate(group[part], axis=1) for part in (0, 1)], axis=0)
                bands.append(from_left(left[parity], stack))
            re = jnp.concatenate([bands[0][:half], bands[1][:half]], axis=0)
            im = jnp.concatenate([bands[0][half:], bands[1][half:]], axis=0)
            plus = jnp.concatenate([re[:, :half] + re[:, half:], im[:, :half] + im[:, half:]], axis=1)
            minus = jnp.concatenate([re[:, :half] - re[:, half:], im[:, :half] - im[:, half:]], axis=1)
            into[p, 0] = from_right(plus, right[0])
            into[p, 1] = from_right(minus, right[1])
            return carry

        lax.fori_loop(0, count, visit, 0, unroll=True)

    def detect(turn, response, start, rate):
        def chunk(i, carry):
            here = pl.ds(pl.multiple_of(start + i * CHUNK, CHUNK), CHUNK)
            for parity in (0, 1):
                span = slice(parity * LANES, (parity + 1) * LANES)
                lin, quad, cubic = (response[j, here, span] for j in range(3))
                sums = [jnp.zeros((CHUNK, LANES), F32)] * 6
                for p in range(count):
                    wr, wi = psi[p, parity, here, :LANES], psi[p, parity, here, LANES:]
                    if rate is not None:
                        wr -= rate * phi[p, parity, here, :LANES]
                        wi -= rate * phi[p, parity, here, LANES:]
                    inten = wr * wr + wi * wi
                    error = inten * (lin + inten * (quad + inten * cubic)) - pats[p, here, span]
                    weight = 2.0 * error * (lin + inten * (2.0 * quad + 3.0 * cubic * inten))
                    squared = inten * inten
                    cubed = squared * inten
                    terms = (error * inten, error * squared, error * cubed,
                             squared, squared * squared, cubed * cubed)
                    sums = [a + b for a, b in zip(sums, terms)]
                    for j, part in ((0, weight * wr), (1, weight * wi)):
                        high, low = split(part)
                        highs[p, parity, here, j * LANES:(j + 1) * LANES] = high
                        lows[p, parity, here, j * LANES:(j + 1) * LANES] = low
                for j in range(6):
                    stats[turn, j, here, span] = sums[j]
            return carry

        lax.fori_loop(0, half // CHUNK, chunk, 0)

    def backward():
        def visit(p, carry):
            _, _, shift = place(p)
            bands = []
            for parity in (0, 1):
                high, low = highs[p, parity], lows[p, parity]
                bands.append(dot(jnp.concatenate([high, low, high], axis=1), right[2 + parity]))
            plus, minus = bands[0] + bands[1], bands[0] - bands[1]
            re = jnp.concatenate([plus[:, :half], minus[:, :half]], axis=1)
            im = jnp.concatenate([plus[:, half:], minus[:, half:]], axis=1)
            bands = []
            for parity in (0, 1):
                rows_in = slice(parity * half, (parity + 1) * half)
                bands.append(from_left(left[2 + parity], jnp.concatenate([re[rows_in], im[rows_in]], axis=0)))
            plus, minus = bands[0] + bands[1], bands[0] - bands[1]
            xr = jnp.concatenate([plus[:half], minus[:half]], axis=0)
            xi = jnp.concatenate([plus[half:], minus[half:]], axis=0)
            pr, pi = probe[0], probe[1]
            keep = lane >= shift
            for part, g in ((0, pr * xr + pi * xi), (1, pr * xi - pi * xr)):
                a = pltpu.roll(g[:, :LANES], shift, axis=1)
                b = pltpu.roll(g[:, LANES:], shift, axis=1)
                zero = jnp.zeros_like(a)
                pads[p, part, 1, pl.ds(width, width), :] = jnp.where(keep, a, zero)
                pads[p, part, 2, pl.ds(width, width), :] = jnp.where(keep, b, a)
                pads[p, part, 3, pl.ds(width, width), :] = jnp.where(keep, zero, b)
            return carry

        lax.fori_loop(0, count, visit, 0, unroll=True)

    def gather(turn, start, length):
        for part in (0, 1):
            for b in range(4):
                total = 0.0
                for p in range(count):
                    oy, block, _ = place(p)
                    total += pads[p, part, b + 1 - block, pl.ds(width - oy + start, length), :]
                grads[turn, part, b, pl.ds(start, length), :] = total

    rows1 = width // 2
    rows2, rows3 = shard.shape[2], z_sums.shape[3]
    cut = rows3 < rows2

    class Sums:
        def __init__(self, turn, old, final):
            self.turn, self.old, self.final = turn, old, final

        def pair(self):
            t = self.turn
            self.first = net.make(stats.at[t, :, at((1 - k) * rows1, rows1), :], half_sums.at[t], row=partner).start()

        def over_cols(self):
            t = self.turn
            self.first.arrived()
            half_sums[t] += stats[t, :, at(k * rows1, rows1), :]
            self.col_copies = []
            for d in range(1, cols):
                other = lax.rem(c + d, cols)
                self.col_copies.append(net.make(half_sums.at[t, :, at(other * rows2, rows2), :],
                                                col_sums.at[t, d - 1], col=other).start())

        def over_z(self):
            t = self.turn
            for copy in self.col_copies:
                copy.arrived()
            shard[t] = half_sums[t, :, at(c * rows2, rows2), :] + sum(col_sums[t, d] for d in range(cols - 1))
            self.z_copies = []
            for d in range(1, depth):
                other = lax.rem(z + d, depth)
                source = shard.at[t, :, at(other * rows3, rows3), :] if cut else shard.at[t]
                self.z_copies.append(net.make(source, z_sums.at[t, d - 1], row=2 * other + k).start())

        def update(self):
            t = self.turn
            for copy in self.z_copies:
                copy.arrived()
            own = shard[t, :, at(z * rows3, rows3), :] if cut else shard[t]
            sums = own + sum(z_sums[t, i] for i in range(depth - 1))
            self.base2 = k * rows1 + c * rows2
            self.base3 = self.base2 + z * rows3 if cut else self.base2
            fresh = self.old[:, at(self.base3, rows3), :] - sums[:3] / (sums[3:] + RIDGE)
            if self.final:
                flat = fresh.reshape(3 * rows3, width)
                fresh = dot(jnp.concatenate(split3(flat), axis=1), right[5]).reshape(3, rows3, width)
            new_coeffs[t, :, at(self.base3, rows3), :] = fresh
            self.back = []
            if cut:
                ready = new_coeffs.at[t, :, at(self.base3, rows3), :]
                for d in range(1, depth):
                    self.back.append(net.make(ready, ready, row=2 * lax.rem(z + d, depth) + k).start())

        def spread(self):
            t = self.turn
            for copy in self.back:
                copy.arrived()
            ready = new_coeffs.at[t, :, at(self.base2, rows2), :]
            self.wide = [net.make(ready, ready, col=lax.rem(c + d, cols)).start() for d in range(1, cols)]

        def swap(self):
            for copy in self.wide:
                copy.arrived()
            ready = new_coeffs.at[self.turn, :, at(k * rows1, rows1), :]
            self.end = net.make(ready, ready, row=partner).start()

        def done(self):
            self.end.arrived()

    class Norm:
        def __init__(self, turn):
            self.turn = turn

        def over_cols(self, square):
            t = self.turn
            sq_mine[t] = square
            self.col_copies = [
                net.make(sq_mine.at[t], sq_cols.at[t, d - 1], col=lax.rem(c + d, cols)).start() for d in range(1, cols)
            ]

        def over_rows(self):
            t = self.turn
            for copy in self.col_copies:
                copy.arrived()
            sq_part[t] = sq_mine[t] + sum(sq_cols[t, d] for d in range(cols - 1))
            self.row_copies = [
                net.make(sq_part.at[t], sq_rows.at[t, d - 1], row=lax.rem(r + d, rows)).start() for d in range(1, rows)
            ]

        def rate(self):
            t = self.turn
            for copy in self.row_copies:
                copy.arrived()
            square = sq_part[t] + sum(sq_rows[t, d] for d in range(rows - 1))
            total = 2.0 * tile * tile * rows * cols
            return STEP_RATE / jnp.sqrt(jnp.sum(square, keepdims=True) / total + EPSILON)

    def fold_rows(turn):
        made = {}
        for which in (1, 0):
            for part in (0, 1):
                made[(which, part)] = net.make(
                    grads.at[turn, part, :, at(edge_row(which), half), :], folds.at[turn, which, part],
                    row=side_dev[which], sends=side_has[which], gets=side_has[which],
                ).start()
        return made

    def add_fold(turn, made, which, part):
        made[(which, part)].arrived()

        def add():
            grads[turn, part, :, at(half + rows_of(which), half), :] += folds[turn, which, part]

        when(side_has[which], add)

    block_x, block_g = 2 * (1 - odd_c), 2 * odd_c

    forward(ext, psi)
    sums0 = Sums(0, coeffs, False)
    detect(0, coeffs, half * (1 - k), None)
    sums0.pair()
    detect(0, coeffs, half * k, None)
    sums0.over_cols()
    backward()
    gather(0, 0, half)
    gather(0, top, half)
    made = fold_rows(0)
    gather(0, half, tile)

    units = [(0, 0), (1, 0), (1, 1), (0, 1)]

    def mid_sources(which, part):
        here = at(half + rows_of(which), half)
        return (grads.at[0, part, pl.ds(block_x, 2), here, :],
                grads.at[0, part, block_g, here, :],
                grads.at[0, part, block_g + 1, here, :])

    def mid_targets(which, part):
        return got_x.at[which, part], got_g.at[which, part, 0], got_g.at[which, part, 1]

    mids = exchange(units, mid_sources, mid_targets, relay_g)
    sides = []

    def take(unit):
        which, part = unit
        here = at(half + rows_of(which), half)
        mids[unit][0].arrived()
        gext[part, pl.ds(block_x, 2), here, :] = grads[0, part, pl.ds(block_x, 2), here, :] + got_x[which, part]
        mids[unit][1].arrived()
        mids[unit][3].arrived()

        @pl.when(has_g)
        def _():
            gext[part, pl.ds(block_g, 2), here, :] = grads[0, part, pl.ds(block_g, 2), here, :] + got_g[which, part]

        @pl.when(jnp.logical_not(has_g))
        def _():
            gext[part, edge_g, here, :] = grads[0, part, edge_g, here, :]

        sides.append(net.make(
            gext.at[part, :, here, :], gext.at[part, :, at(side_row(which), half), :],
            row=side_dev[which], sends=side_has[which], gets=side_has[which],
        ).start())

    add_fold(0, made, *units[0])
    push(mids[units[0]])
    add_fold(0, made, *units[1])
    push(mids[units[1]])
    hand_on(mids[units[0]])
    add_fold(0, made, *units[2])
    push(mids[units[2]])
    hand_on(mids[units[1]])
    add_fold(0, made, *units[3])
    push(mids[units[3]])
    sums0.over_z()
    hand_on(mids[units[2]])
    take(units[0])
    sums0.update()
    hand_on(mids[units[3]])
    take(units[1])
    sums0.spread()
    take(units[2])
    take(units[3])
    sums0.swap()

    def squares(blocks):
        total = 0.0
        for block in blocks:
            total += jnp.sum((block * block).reshape(-1, 8, LANES), axis=0)
        return total

    norm0 = Norm(0)
    norm0.over_cols(squares([gext[part, b, inner, :] for part in (0, 1) for b in (1, 2)]))
    for copy in sides:
        copy.arrived()
    norm0.over_rows()

    forward(gext, phi)
    rate0 = norm0.rate()
    sums0.done()
    sums1 = Sums(1, new_coeffs.at[0], True)
    detect(1, new_coeffs.at[0], half * (1 - k), rate0)
    sums1.pair()
    detect(1, new_coeffs.at[0], half * k, rate0)
    sums1.over_cols()
    backward()
    gather(1, 0, half)
    gather(1, top, half)
    made = fold_rows(1)
    gather(1, half, tile)

    units = [(0, 0), (0, 1), (1, 0), (1, 1)]

    def last_sources(which, part):
        start = half + rows_of(which)
        return (grads.at[1, part, out_x, at(start, half), :],
                grads.at[1, part, out_g, at(start, quarter), :],
                grads.at[1, part, out_g, at(start + quarter, quarter), :])

    def last_targets(which, part):
        return (last_x.at[which, part], last_g.at[which, part, pl.ds(0, quarter), :],
                last_g.at[which, part, pl.ds(quarter, quarter), :])

    lasts = exchange(units, last_sources, last_targets, relay_last)
    for part in (0, 1):
        for b in (0, 1):
            base[part, b] = ext[part, 1 + b, inner, :] - rate0 * gext[part, 1 + b, inner, :]
    for n, unit in enumerate(units):
        add_fold(1, made, *unit)
        push(lasts[unit])
        if n:
            hand_on(lasts[units[n - 1]])
    hand_on(lasts[units[3]])
    sums1.over_z()
    square = 0.0
    for which, part in units:
        here = at(half + rows_of(which), half)
        there = at(rows_of(which), half)
        lasts[(which, part)][0].arrived()
        lasts[(which, part)][1].arrived()
        lasts[(which, part)][3].arrived()
        mine = grads[1, part, edge_x, here, :] + last_x[which, part]
        gtile[part, edge_x - 1, there, :] = mine
        square += squares([mine])

        @pl.when(has_g)
        def _():
            gtile[part, edge_g - 1, there, :] = grads[1, part, edge_g, here, :] + last_g[which, part]

        @pl.when(jnp.logical_not(has_g))
        def _():
            gtile[part, edge_g - 1, there, :] = grads[1, part, edge_g, here, :]

        square += squares([gtile[part, edge_g - 1, there, :]])
    norm1 = Norm(1)
    norm1.over_cols(square)
    sums1.update()
    norm1.over_rows()
    sums1.spread()
    rate1 = norm1.rate()
    for part in (0, 1):
        for b in (0, 1):
            field_out[part, :, b * LANES:(b + 1) * LANES] = base[part, b] - rate1 * gtile[part, b]
    sums1.swap()
    sums1.done()
    for i in range(3):
        for b in (0, 1):
            span = slice(b * LANES, (b + 1) * LANES)
            for parity in (0, 1):
                woven[i, b, pl.ds(parity, half, stride=2), :] = new_coeffs[1, i, parity * half:(parity + 1) * half, span]
            coeffs_out[i, :, span] = woven[i, b]
    net.finish()


def local(object_field, probe, coeffs, patterns, offsets):
    rows, cols = lax.axis_size("row"), lax.axis_size("col")
    depth = rows // 2
    count, width = patterns.shape[2], probe.shape[1]
    half = width // 2
    tile = object_field.shape[1]
    size = tile + width
    rows1 = width // 2
    rows2 = rows1 // cols
    rows3 = rows2 // depth if rows2 % (8 * depth) == 0 else rows2
    left, right = dft_halves(width)
    vmem = pl.BlockSpec(memory_space=pltpu.VMEM)
    hbm = pl.BlockSpec(memory_space=pl.ANY)
    semaphores = copies_needed(rows, cols)
    extended = (2, size // LANES, size, LANES)
    freq = (count, 2, width, width)
    return pl.pallas_call(
        refine_kernel,
        out_shape=(
            jax.ShapeDtypeStruct((2, tile, tile), F32),
            jax.ShapeDtypeStruct(coeffs.shape, F32),
        ),
        in_specs=[hbm] * 4 + [pl.BlockSpec(memory_space=pltpu.SMEM)] + [hbm] * 2,
        out_specs=(vmem, vmem),
        scratch_shapes=[
            pltpu.VMEM(extended, F32),
            pltpu.VMEM((2,) + extended, F32),
            pltpu.VMEM(extended, F32),
            pltpu.VMEM((count, 2, 5, 3 * width, LANES), F32),
            pltpu.VMEM(freq, F32),
            pltpu.VMEM(freq, F32),
            pltpu.VMEM(freq, BF16),
            pltpu.VMEM(freq, BF16),
            pltpu.VMEM((2, width, width), F32),
            pltpu.VMEM((3, width, width), F32),
            pltpu.VMEM((count, width, width), F32),
            pltpu.VMEM((count, width, width), F32),
            pltpu.VMEM(left.shape, BF16),
            pltpu.VMEM(right.shape, BF16),
            pltpu.VMEM((2, 6, width, width), F32),
            pltpu.VMEM((2, 6, rows1, width), F32),
            pltpu.VMEM((2, cols - 1, 6, rows2, width), F32),
            pltpu.VMEM((2, 6, rows2, width), F32),
            pltpu.VMEM((2, depth - 1, 6, rows3, width), F32),
            pltpu.VMEM((3, 3, width, width), F32),
            pltpu.VMEM((2, 2, 2, size // LANES, half, LANES), F32),
            pltpu.VMEM((2, 2, 2, half, LANES), F32),
            pltpu.VMEM((2, 2, 2, half, LANES), F32),
            pltpu.VMEM((4, half // 2, LANES), F32),
            pltpu.VMEM((4, half, LANES), F32),
            pltpu.VMEM((2, 2, half, LANES), F32),
            pltpu.VMEM((2, 2, half, LANES), F32),
            pltpu.VMEM((4, half // 2, LANES), F32),
            pltpu.VMEM((2, 2, tile, LANES), F32),
            pltpu.VMEM((2, 2, tile, LANES), F32),
            pltpu.VMEM((2, 8, LANES), F32),
            pltpu.VMEM((2, cols - 1, 8, LANES), F32),
            pltpu.VMEM((2, 8, LANES), F32),
            pltpu.VMEM((2, rows - 1, 8, LANES), F32),
            pltpu.VMEM((3, width // LANES, width, LANES), F32),
            pltpu.SemaphoreType.DMA((8,)),
            pltpu.SemaphoreType.DMA((semaphores,)),
            pltpu.SemaphoreType.DMA((semaphores,)),
        ],
        compiler_params=pltpu.CompilerParams(
            collective_id=0, has_side_effects=True, vmem_limit_bytes=58 * 1024 * 1024
        ),
        name="refine",
    )(object_field, probe, coeffs, patterns, offsets, left, right)


def solution(mesh):
    placed = (
        P(None, "row", "col"),
        P(),
        P(),
        P("row", "col", None, None, None),
        P("row", "col", None, None),
    )
    return jax.shard_map(
        local, mesh=mesh, in_specs=placed, out_specs=(P(None, "row", "col"), P()), check_vma=False
    )
```

```python
import functools

import jax
import jax.numpy as jnp
import ml_dtypes
import numpy as np
from jax import lax
from jax.experimental import pallas as pl
from jax.experimental.pallas import tpu as pltpu
from jax.sharding import PartitionSpec as P

STEP_RATE = 0.2
RIDGE = 1.0
EPSILON = 1e-06
LANES = 128
CHUNK = 16
F32 = jnp.float32
BF16 = jnp.bfloat16


def dft_halves(order):
    half = order // 2
    index = np.arange(order)
    angle = -2.0 * np.pi / order * (index[:, None] * index[None, :] % order)
    real, imag = np.cos(angle) / np.sqrt(order), np.sin(angle) / np.sqrt(order)
    lefts, rights = [], []
    for parity in (0, 1):
        re, im = real[parity::2, :half], imag[parity::2, :half]
        full = np.block([[re, -im], [im, re]]).astype(np.float32)
        for into, forward in ((lefts, full), (rights, full.T)):
            high = forward.astype(ml_dtypes.bfloat16)
            low = (forward - high.astype(np.float32)).astype(ml_dtypes.bfloat16)
            into.append((high, low))
    wide = lambda pair: np.concatenate([pair[0], pair[0], pair[1]], axis=1)
    tall = lambda pair: np.concatenate([pair[0], pair[0], pair[1]], axis=0)
    on_left = [wide(m) for m in lefts] + [wide(m) for m in rights]
    on_right = [tall(m) for m in rights] + [tall(m) for m in lefts]
    order_of = np.concatenate([index[0::2], index[1::2]])
    perm = (order_of[:, None] == index[None, :]).astype(ml_dtypes.bfloat16)
    on_left.append(np.concatenate([perm] * 3, axis=1))
    on_right.append(np.concatenate([perm.T] * 3, axis=0))
    on_right.append(np.concatenate([perm] * 3, axis=0))
    return jnp.asarray(np.stack(on_left)), jnp.asarray(np.stack(on_right))


def dot(left, right):
    return jnp.dot(left, right, preferred_element_type=F32)


def split(full):
    high = full.astype(BF16)
    return high, (full - high.astype(F32)).astype(BF16)


def split3(full):
    high = full.astype(BF16)
    rest = full - high.astype(F32)
    mid = rest.astype(BF16)
    return high, mid, (rest - mid.astype(F32)).astype(BF16)


def from_left(matrix, full):
    high, low = split(full)
    return dot(matrix, jnp.concatenate([high, low, high], axis=0))


def from_right(full, matrix):
    high, low = split(full)
    return dot(jnp.concatenate([high, low, high], axis=1), matrix)


class Copies:
    def __init__(self, send, recv):
        self.send, self.recv, self.used, self.made, self.ended = send, recv, 0, [], 0

    def make(self, source, target, row=None, col=None, sends=None, gets=None):
        slot = self.used
        self.used += 1
        where = (lax.axis_index("row") if row is None else row, lax.axis_index("col") if col is None else col)
        copy = pltpu.make_async_remote_copy(
            src_ref=source, dst_ref=target, send_sem=self.send.at[slot], recv_sem=self.recv.at[slot],
            device_id=where, device_id_type=pl.DeviceIdType.MESH,
        )
        made = Copy(copy, sends, gets)
        self.made.append(made)
        return made

    def finish(self, mark=None):
        mark = len(self.made) if mark is None else mark
        for made in self.made[self.ended:mark]:
            made.sent()
        self.ended = mark


def when(condition, act):
    if condition is None:
        act()
    else:
        pl.when(condition)(act)


class Copy:
    def __init__(self, copy, sends, gets):
        self.copy, self.sends, self.gets = copy, sends, gets

    def start(self):
        when(self.sends, self.copy.start)
        return self

    def arrived(self):
        when(self.gets, self.copy.wait_recv)

    def sent(self):
        when(self.sends, self.copy.wait_send)


def both(a, b):
    return b if a is None else a if b is None else a & b


def copies_needed(rows, cols):
    return 160 + 4 * (rows + cols) + rows * cols


def refine_kernel(field_hbm, probe_hbm, coeffs_hbm, pats_hbm, offs, left_hbm, right_hbm,
                  field_out, coeffs_out,
                  ext, grads, gext, pads, psi, phi, highs, lows, probe, coeffs, pats, left, right,
                  stats, half_sums, col_sums, shard, z_sums, new_coeffs,
                  folds, got_x, got_g, relay_in, relay_g, last_x, last_g, relay_last, base, gtile,
                  sq_mine, sq_pair, sq_part, sq_all, woven, acc,
                  local_sem, send_sem, recv_sem):
    rows, cols = lax.axis_size("row"), lax.axis_size("col")
    r, c = lax.axis_index("row"), lax.axis_index("col")
    depth = rows // 2
    k, z = lax.rem(r, 2), lax.div(r, 2)
    count = pats.shape[0]
    width = probe.shape[1]
    half = width // 2
    size = ext.shape[2]
    tile = size - width
    top = half + tile
    net = Copies(send_sem, recv_sem)

    partner = r + 1 - 2 * k
    beyond = r - 1 + 2 * k
    has_z = (beyond >= 0) & (beyond < rows)
    beyond = lax.rem(beyond + rows, rows)
    odd_c = lax.rem(c, 2)
    step_g = 2 * odd_c - 1
    has_g = (c + step_g >= 0) & (c + step_g < cols)
    has_r = (c - 2 * step_g >= 0) & (c - 2 * step_g < cols)
    col_x = c - step_g
    col_g = lax.rem(c + step_g + cols, cols)
    col_r = lax.rem(c + 2 * step_g + 2 * cols, cols)

    def chip(dz, dc):
        return 2 * lax.rem(z + dz, depth) + k, lax.rem(c + dc, cols)

    others = [(dz, dc) for dz in range(depth) for dc in range(cols) if dz or dc]

    barrier = pltpu.get_barrier_semaphore()

    def greet(row, col):
        pl.semaphore_signal(barrier, inc=1, device_id=(row, col), device_id_type=pl.DeviceIdType.MESH)

    for dz, dc in others:
        greet(*chip(dz, dc))
    greet(partner, c)
    when(has_z, lambda: greet(beyond, c))
    greeted = len(others) + 1 + has_z.astype(jnp.int32)

    inner = pl.ds(half, tile)
    loads = []

    def load(source, target):
        copy = pltpu.make_async_copy(source, target, local_sem.at[len(loads)])
        copy.start()
        loads.append(copy)
        return copy

    field_loads = [
        load(field_hbm.at[:, :, pl.ds(b * LANES, LANES)], ext.at[:, 1 + b, inner, :]) for b in (0, 1)
    ]
    pats_load = load(pats_hbm.at[0, 0], pats)
    coeffs_load = load(coeffs_hbm, acc)
    left_load = load(left_hbm, left)
    right_load = load(right_hbm, right)
    probe_load = load(probe_hbm, probe)

    for edge, b in ((c == 0, 0), (c == cols - 1, 3)):
        @pl.when(edge)
        def _():
            ext[:, b] = jnp.zeros((2, size, LANES), F32)
            gext[:, b] = jnp.zeros((2, size, LANES), F32)
    for edge, start in ((r == 0, 0), (r == rows - 1, top)):
        @pl.when(edge)
        def _():
            ext[:, :, pl.ds(start, half), :] = jnp.zeros((2, 4, half, LANES), F32)
            gext[:, :, pl.ds(start, half), :] = jnp.zeros((2, 4, half, LANES), F32)

    def clear(p, carry):
        for part in (0, 1):
            for b in (0, 4):
                pads[p, part, b] = jnp.zeros((3 * width, LANES), F32)
            for b in (1, 2, 3):
                for start in (0, 2 * width):
                    pads[p, part, b, pl.ds(start, width), :] = jnp.zeros((width, LANES), F32)
        return carry

    lax.fori_loop(0, count, clear, 0)
    for copy in field_loads:
        copy.wait()
    pl.semaphore_wait(barrier, greeted)

    def rows_of(which):
        return half * (1 - k) if which == 0 else half * k

    def side_row(which):
        return top * k if which == 0 else top * (1 - k)

    def edge_row(which):
        return top * (1 - k) if which == 0 else top * k

    def at(start, length):
        return pl.ds(pl.multiple_of(start, 8), length)

    side_dev = (partner, beyond)
    side_has = (None, has_z)

    ends = []
    for which in (1, 0):
        mine = at(half + rows_of(which), half)
        there = at(side_row(which), half)
        ends.append(net.make(ext.at[:, pl.ds(1, 2), mine, :], ext.at[:, pl.ds(1, 2), there, :],
                             row=side_dev[which], sends=side_has[which], gets=side_has[which]).start())

    edge_x, edge_g = 2 - odd_c, 1 + odd_c
    out_x, out_g = 3 * (1 - odd_c), 3 * odd_c
    far_x, far_g = 3 * odd_c, 3 * (1 - odd_c)
    quarter = half // 2
    first_units = [(1, 0), (1, 1), (0, 0), (0, 1)]

    def exchange(units, sources, targets, relays):
        made = {}
        for n, unit in enumerate(units):
            sx, sg1, sg2 = sources(*unit)
            tx, tg1, tg2 = targets(*unit)
            made[unit] = (
                net.make(sx, tx, col=col_x),
                net.make(sg1, tg1, col=col_g, sends=has_g, gets=has_g),
                net.make(sg2, relays.at[n], col=col_r, sends=has_g, gets=has_r),
                net.make(relays.at[n], tg2, col=col_x, sends=has_r, gets=has_g),
            )
        return made

    def push(copies):
        copies[2].start()
        copies[0].start()
        copies[1].start()

    def hand_on(copies):
        copies[2].arrived()
        copies[3].start()

    def first_sources(which, part):
        start = half + rows_of(which)
        return (ext.at[part, edge_x, at(start, half), :],
                ext.at[part, edge_g, at(start, quarter), :],
                ext.at[part, edge_g, at(start + quarter, quarter), :])

    def first_targets(which, part):
        start = half + rows_of(which)
        return (ext.at[part, far_x, at(start, half), :],
                ext.at[part, far_g, at(start, quarter), :],
                ext.at[part, far_g, at(start + quarter, quarter), :])

    side = exchange(first_units, first_sources, first_targets, relay_in)
    def straight(unit):
        side[unit][0].start()
        side[unit][1].start()

    for unit in first_units:
        side[unit][2].start()
    for unit in first_units[:3]:
        straight(unit)

    def reorder(full):
        part = dot(jnp.concatenate(split3(full), axis=1), right[4])
        return dot(left[4], jnp.concatenate(split3(part), axis=0))

    def reorder_pats(p, carry):
        pats[p] = reorder(pats[p])
        return carry

    for copy in (pats_load, left_load, right_load, coeffs_load, probe_load):
        copy.wait()
    lax.fori_loop(0, count // 2, reorder_pats, 0)
    hand_on(side[first_units[0]])
    hand_on(side[first_units[1]])
    straight(first_units[3])
    lax.fori_loop(count // 2, count, reorder_pats, 0)
    hand_on(side[first_units[2]])
    hand_on(side[first_units[3]])
    for i in range(3):
        full = reorder(acc[i])
        for parity in (0, 1):
            coeffs[parity, i] = full[:, parity * LANES:(parity + 1) * LANES]

    corners = []

    def corner(unit, arrivals, b, has):
        which, part = unit
        for i in arrivals:
            side[unit][i].arrived()
        cond = both(has, side_has[which])
        mine = at(half + rows_of(which), half)
        there = at(side_row(which), half)
        corners.append(net.make(ext.at[part, b, mine, :], ext.at[part, b, there, :],
                                row=side_dev[which], sends=cond, gets=cond).start())

    for pair in (first_units[:2], first_units[2:]):
        for unit in pair:
            corner(unit, (0,), out_x, None)
        for unit in pair:
            corner(unit, (1, 3), out_g, has_g)
    for copy in ends + corners:
        copy.arrived()

    lane = lax.broadcasted_iota(jnp.int32, (1, LANES), 1)

    def place(p):
        oy, ox = offs[0, 0, 0, p], offs[0, 0, 1, p]
        block = lax.div(ox, LANES)
        return oy, block, ox - block * LANES

    def forward(source, into):
        def visit(p, carry):
            oy, block, shift = place(p)
            window = []
            keep = lane < LANES - shift
            for part in (0, 1):
                turned = [
                    pltpu.roll(source[part, block + j, pl.ds(oy, width), :], lax.rem(LANES - shift, LANES), axis=1)
                    for j in range(3)
                ]
                window.append([jnp.where(keep, turned[j], turned[j + 1]) for j in (0, 1)])
            sums, difs = [[], []], [[], []]
            for h in (0, 1):
                pr, pi = probe[0, :, h * LANES:(h + 1) * LANES], probe[1, :, h * LANES:(h + 1) * LANES]
                wr, wi = window[0][h], window[1][h]
                for part, x in ((0, pr * wr - pi * wi), (1, pr * wi + pi * wr)):
                    sums[part].append(x[:half] + x[half:])
                    difs[part].append(x[:half] - x[half:])
            bands = []
            for parity, group in ((0, sums), (1, difs)):
                stack = jnp.concatenate([jnp.concatenate(group[part], axis=1) for part in (0, 1)], axis=0)
                bands.append(from_left(left[parity], stack))
            re = jnp.concatenate([bands[0][:half], bands[1][:half]], axis=0)
            im = jnp.concatenate([bands[0][half:], bands[1][half:]], axis=0)
            plus = jnp.concatenate([re[:, :half] + re[:, half:], im[:, :half] + im[:, half:]], axis=1)
            minus = jnp.concatenate([re[:, :half] - re[:, half:], im[:, :half] - im[:, half:]], axis=1)
            into[p, 0] = from_right(plus, right[0])
            into[p, 1] = from_right(minus, right[1])
            return carry

        lax.fori_loop(0, count, visit, 0, unroll=True)

    def detect(turn, parity, response, rate):
        span = slice(parity * LANES, (parity + 1) * LANES)

        def chunk(i, carry):
            here = pl.ds(pl.multiple_of(i * CHUNK, CHUNK), CHUNK)
            lin, quad, cubic = (response[parity, j, here, :] for j in range(3))
            sums = [jnp.zeros((CHUNK, LANES), F32)] * 6
            for p in range(count):
                wr, wi = psi[p, parity, here, :LANES], psi[p, parity, here, LANES:]
                if rate is not None:
                    wr -= rate * phi[p, parity, here, :LANES]
                    wi -= rate * phi[p, parity, here, LANES:]
                inten = wr * wr + wi * wi
                error = inten * (lin + inten * (quad + inten * cubic)) - pats[p, here, span]
                weight = 2.0 * error * (lin + inten * (2.0 * quad + 3.0 * cubic * inten))
                squared = inten * inten
                cubed = squared * inten
                terms = (error * inten, error * squared, error * cubed,
                         squared, squared * squared, cubed * cubed)
                sums = [a + b for a, b in zip(sums, terms)]
                for j, part in ((0, weight * wr), (1, weight * wi)):
                    high, low = split(part)
                    highs[p, parity, here, j * LANES:(j + 1) * LANES] = high
                    lows[p, parity, here, j * LANES:(j + 1) * LANES] = low
            for j in range(6):
                stats[turn, parity, j, here, :] = sums[j]
            return carry

        lax.fori_loop(0, width // CHUNK, chunk, 0, unroll=2)

    def backward():
        def visit(p, carry):
            _, _, shift = place(p)
            bands = []
            for parity in (0, 1):
                high, low = highs[p, parity], lows[p, parity]
                bands.append(dot(jnp.concatenate([high, low, high], axis=1), right[2 + parity]))
            plus, minus = bands[0] + bands[1], bands[0] - bands[1]
            re = jnp.concatenate([plus[:, :half], minus[:, :half]], axis=1)
            im = jnp.concatenate([plus[:, half:], minus[:, half:]], axis=1)
            bands = []
            for parity in (0, 1):
                rows_in = slice(parity * half, (parity + 1) * half)
                bands.append(from_left(left[2 + parity], jnp.concatenate([re[rows_in], im[rows_in]], axis=0)))
            plus, minus = bands[0] + bands[1], bands[0] - bands[1]
            xr = jnp.concatenate([plus[:half], minus[:half]], axis=0)
            xi = jnp.concatenate([plus[half:], minus[half:]], axis=0)
            pr, pi = probe[0], probe[1]
            keep = lane >= shift
            for part, g in ((0, pr * xr + pi * xi), (1, pr * xi - pi * xr)):
                a = pltpu.roll(g[:, :LANES], shift, axis=1)
                b = pltpu.roll(g[:, LANES:], shift, axis=1)
                zero = jnp.zeros_like(a)
                pads[p, part, 1, pl.ds(width, width), :] = jnp.where(keep, a, zero)
                pads[p, part, 2, pl.ds(width, width), :] = jnp.where(keep, b, a)
                pads[p, part, 3, pl.ds(width, width), :] = jnp.where(keep, zero, b)
            return carry

        lax.fori_loop(0, count, visit, 0, unroll=True)

    def gather(turn, start, length):
        for part in (0, 1):
            for b in range(4):
                total = 0.0
                for p in range(count):
                    oy, block, _ = place(p)
                    total += pads[p, part, b + 1 - block, pl.ds(width - oy + start, length), :]
                grads[turn, part, b, pl.ds(start, length), :] = total

    rows1 = width // 2
    rows2, rows3 = shard.shape[3], z_sums.shape[4]
    cut = rows3 < rows2

    class Sums:
        def __init__(self, turn, parity, old):
            self.at, self.old = (turn, parity), old
            self.base2 = k * rows1 + c * rows2
            self.base3 = self.base2 + z * rows3 if cut else self.base2

        def pair(self):
            t = self.at
            self.first = net.make(stats.at[*t, :, at((1 - k) * rows1, rows1), :], half_sums.at[t], row=partner).start()

        def over_cols(self):
            t = self.at
            self.first.arrived()
            half_sums[t] += stats[*t, :, at(k * rows1, rows1), :]
            self.copies = []
            for d in range(1, cols):
                other = lax.rem(c + d, cols)
                self.copies.append(net.make(half_sums.at[*t, :, at(other * rows2, rows2), :],
                                            col_sums.at[*t, d - 1], col=other).start())

        def over_z(self):
            t = self.at
            for copy in self.copies:
                copy.arrived()
            shard[t] = half_sums[*t, :, at(c * rows2, rows2), :] + sum(col_sums[*t, d] for d in range(cols - 1))
            self.copies = []
            for d in range(1, depth):
                other = lax.rem(z + d, depth)
                source = shard.at[*t, :, at(other * rows3, rows3), :] if cut else shard.at[t]
                self.copies.append(net.make(source, z_sums.at[*t, d - 1], row=2 * other + k).start())

        def update(self):
            t = self.at
            for copy in self.copies:
                copy.arrived()
            own = shard[*t, :, at(z * rows3, rows3), :] if cut else shard[t]
            sums = own + sum(z_sums[*t, i] for i in range(depth - 1))
            new_coeffs[*t, :, at(self.base3, rows3), :] = (
                self.old[t[1], :, at(self.base3, rows3), :] - sums[:3] / (sums[3:] + RIDGE))
            self.copies = []
            if cut:
                ready = new_coeffs.at[*t, :, at(self.base3, rows3), :]
                for d in range(1, depth):
                    self.copies.append(net.make(ready, ready, row=2 * lax.rem(z + d, depth) + k).start())

        def spread(self):
            for copy in self.copies:
                copy.arrived()
            ready = new_coeffs.at[*self.at, :, at(self.base2, rows2), :]
            self.copies = [net.make(ready, ready, col=lax.rem(c + d, cols)).start() for d in range(1, cols)]

        def swap(self):
            for copy in self.copies:
                copy.arrived()
            ready = new_coeffs.at[*self.at, :, at(k * rows1, rows1), :]
            self.end = net.make(ready, ready, row=partner).start()

        def done(self):
            self.end.arrived()

    class Norm:
        def __init__(self, turn):
            self.turn = turn

        def pair(self, square):
            t = self.turn
            sq_mine[t] = square
            self.first = net.make(sq_mine.at[t], sq_pair.at[t], row=partner).start()

        def wide(self):
            t = self.turn
            self.first.arrived()
            sq_part[t] = sq_mine[t] + sq_pair[t]
            self.copies = []
            for i, place in enumerate(others):
                row, col = chip(*place)
                self.copies.append(net.make(sq_part.at[t], sq_all.at[t, i], row=row, col=col).start())

        def rate(self):
            t = self.turn
            for copy in self.copies:
                copy.arrived()
            square = sq_part[t] + sum(sq_all[t, i] for i in range(len(others)))
            total = 2.0 * tile * tile * rows * cols
            return STEP_RATE / jnp.sqrt(jnp.sum(square, keepdims=True) / total + EPSILON)

    def fold_rows(turn):
        made = {}
        for which in (1, 0):
            for part in (0, 1):
                made[(which, part)] = net.make(
                    grads.at[turn, part, :, at(edge_row(which), half), :], folds.at[turn, which, part],
                    row=side_dev[which], sends=side_has[which], gets=side_has[which],
                ).start()
        return made

    def add_fold(turn, made, which, part):
        made[(which, part)].arrived()

        def add():
            grads[turn, part, :, at(half + rows_of(which), half), :] += folds[turn, which, part]

        when(side_has[which], add)

    block_x, block_g = 2 * (1 - odd_c), 2 * odd_c

    forward(ext, psi)
    sums0 = [Sums(0, parity, coeffs) for parity in (0, 1)]
    detect(0, 0, coeffs, None)
    sums0[0].pair()
    detect(0, 1, coeffs, None)
    sums0[1].pair()
    sums0[0].over_cols()
    sums0[1].over_cols()
    backward()
    gather(0, 0, half)
    gather(0, top, half)
    made = fold_rows(0)
    gather(0, half, tile)

    units = [(0, 0), (1, 0), (1, 1), (0, 1)]

    def mid_sources(which, part):
        here = at(half + rows_of(which), half)
        return (grads.at[0, part, pl.ds(block_x, 2), here, :],
                grads.at[0, part, block_g, here, :],
                grads.at[0, part, block_g + 1, here, :])

    def mid_targets(which, part):
        return got_x.at[which, part], got_g.at[which, part, 0], got_g.at[which, part, 1]

    mids = exchange(units, mid_sources, mid_targets, relay_g)
    sides = []

    def take(unit):
        which, part = unit
        here = at(half + rows_of(which), half)
        mids[unit][0].arrived()
        gext[part, pl.ds(block_x, 2), here, :] = grads[0, part, pl.ds(block_x, 2), here, :] + got_x[which, part]
        mids[unit][1].arrived()
        mids[unit][3].arrived()

        @pl.when(has_g)
        def _():
            gext[part, pl.ds(block_g, 2), here, :] = grads[0, part, pl.ds(block_g, 2), here, :] + got_g[which, part]

        @pl.when(jnp.logical_not(has_g))
        def _():
            gext[part, edge_g, here, :] = grads[0, part, edge_g, here, :]

        sides.append(net.make(
            gext.at[part, :, here, :], gext.at[part, :, at(side_row(which), half), :],
            row=side_dev[which], sends=side_has[which], gets=side_has[which],
        ).start())

    for unit in units:
        add_fold(0, made, *unit)
        push(mids[unit])
    sums0[0].over_z()
    hand_on(mids[units[0]])
    hand_on(mids[units[1]])
    sums0[1].over_z()
    hand_on(mids[units[2]])
    sums0[0].update()
    hand_on(mids[units[3]])
    take(units[0])
    sums0[1].update()
    take(units[1])
    sums0[0].spread()
    take(units[2])
    sums0[1].spread()
    take(units[3])

    def squares(blocks):
        total = 0.0
        for block in blocks:
            total += jnp.sum((block * block).reshape(-1, 8, LANES), axis=0)
        return total

    norm0 = Norm(0)
    mark = len(net.made)
    norm0.pair(squares([gext[part, b, inner, :] for part in (0, 1) for b in (1, 2)]))
    for copy in sides:
        copy.arrived()
    norm0.wide()

    forward(gext, phi)
    net.finish(mark)
    sums0[0].swap()
    rate0 = norm0.rate()
    sums0[0].done()
    sums1 = [Sums(1, parity, new_coeffs.at[0]) for parity in (0, 1)]
    detect(1, 0, new_coeffs.at[0], rate0)
    sums0[1].swap()
    sums1[0].pair()
    sums0[1].done()
    detect(1, 1, new_coeffs.at[0], rate0)
    sums1[1].pair()
    sums1[0].over_cols()
    sums1[1].over_cols()
    backward()
    gather(1, 0, half)
    gather(1, top, half)
    made = fold_rows(1)
    gather(1, half, tile)

    units = [(0, 0), (0, 1), (1, 0), (1, 1)]

    def last_sources(which, part):
        start = half + rows_of(which)
        return (grads.at[1, part, out_x, at(start, half), :],
                grads.at[1, part, out_g, at(start, quarter), :],
                grads.at[1, part, out_g, at(start + quarter, quarter), :])

    def last_targets(which, part):
        return (last_x.at[which, part], last_g.at[which, part, pl.ds(0, quarter), :],
                last_g.at[which, part, pl.ds(quarter, quarter), :])

    lasts = exchange(units, last_sources, last_targets, relay_last)
    for part in (0, 1):
        for b in (0, 1):
            base[part, b] = ext[part, 1 + b, inner, :] - rate0 * gext[part, 1 + b, inner, :]
    def settle(unit):
        which, part = unit
        here = at(half + rows_of(which), half)
        there = at(rows_of(which), half)
        lasts[(which, part)][0].arrived()
        lasts[(which, part)][1].arrived()
        lasts[(which, part)][3].arrived()
        mine = grads[1, part, edge_x, here, :] + last_x[which, part]
        gtile[part, edge_x - 1, there, :] = mine
        square = squares([mine])

        @pl.when(has_g)
        def _():
            gtile[part, edge_g - 1, there, :] = grads[1, part, edge_g, here, :] + last_g[which, part]

        @pl.when(jnp.logical_not(has_g))
        def _():
            gtile[part, edge_g - 1, there, :] = grads[1, part, edge_g, here, :]

        return square + squares([gtile[part, edge_g - 1, there, :]])

    for unit in units[:2]:
        add_fold(1, made, *unit)
        push(lasts[unit])
    sums1[0].over_z()
    hand_on(lasts[units[0]])
    add_fold(1, made, *units[2])
    push(lasts[units[2]])
    hand_on(lasts[units[1]])
    add_fold(1, made, *units[3])
    push(lasts[units[3]])
    sums1[1].over_z()
    hand_on(lasts[units[2]])
    sums1[0].update()
    hand_on(lasts[units[3]])
    square = settle(units[0])
    sums1[1].update()
    square += settle(units[1])
    sums1[0].spread()
    mark = len(net.made) - 2 * (cols - 1)
    square += settle(units[2])
    square += settle(units[3])
    norm1 = Norm(1)
    norm1.pair(square)
    sums1[1].spread()
    norm1.wide()
    net.finish(mark)
    rate1 = norm1.rate()
    for part in (0, 1):
        for b in (0, 1):
            field_out[part, :, b * LANES:(b + 1) * LANES] = base[part, b] - rate1 * gtile[part, b]
    sums1[0].swap()
    sums1[0].done()

    def natural(i, parity):
        begin = parity * LANES
        spread = jnp.concatenate([right[5, j * width + begin:j * width + begin + LANES, :] for j in range(3)], axis=0)
        return dot(jnp.concatenate(split3(new_coeffs[1, parity, i]), axis=1), spread)

    for i in range(3):
        acc[i] = natural(i, 0)
    sums1[1].swap()
    sums1[1].done()
    for i in range(3):
        full = acc[i] + natural(i, 1)
        for b in (0, 1):
            span = slice(b * LANES, (b + 1) * LANES)
            for parity in (0, 1):
                woven[i, b, pl.ds(parity, half, stride=2), :] = full[parity * half:(parity + 1) * half, span]
            coeffs_out[i, :, span] = woven[i, b]
    net.finish()


def local(object_field, probe, coeffs, patterns, offsets):
    rows, cols = lax.axis_size("row"), lax.axis_size("col")
    depth = rows // 2
    count, width = patterns.shape[2], probe.shape[1]
    half = width // 2
    tile = object_field.shape[1]
    size = tile + width
    rows1 = width // 2
    rows2 = rows1 // cols
    rows3 = rows2 // depth if rows2 % (8 * depth) == 0 else rows2
    left, right = dft_halves(width)
    vmem = pl.BlockSpec(memory_space=pltpu.VMEM)
    hbm = pl.BlockSpec(memory_space=pltpu.HBM)
    semaphores = copies_needed(rows, cols)
    extended = (2, size // LANES, size, LANES)
    freq = (count, 2, width, width)
    refined = pl.pallas_call(
        refine_kernel,
        out_shape=(
            jax.ShapeDtypeStruct((2, tile, tile), F32),
            jax.ShapeDtypeStruct(coeffs.shape, F32),
        ),
        in_specs=[hbm] * 4 + [pl.BlockSpec(memory_space=pltpu.SMEM)] + [hbm] * 2,
        out_specs=(vmem, vmem),
        scratch_shapes=[
            pltpu.VMEM(extended, F32),
            pltpu.VMEM((2,) + extended, F32),
            pltpu.VMEM(extended, F32),
            pltpu.VMEM((count, 2, 5, 3 * width, LANES), F32),
            pltpu.VMEM(freq, F32),
            pltpu.VMEM(freq, F32),
            pltpu.VMEM(freq, BF16),
            pltpu.VMEM(freq, BF16),
            pltpu.VMEM((2, width, width), F32),
            pltpu.VMEM((2, 3, width, LANES), F32),
            pltpu.VMEM((count, width, width), F32),
            pltpu.VMEM(left.shape, BF16),
            pltpu.VMEM(right.shape, BF16),
            pltpu.VMEM((2, 2, 6, width, LANES), F32),
            pltpu.VMEM((2, 2, 6, rows1, LANES), F32),
            pltpu.VMEM((2, 2, cols - 1, 6, rows2, LANES), F32),
            pltpu.VMEM((2, 2, 6, rows2, LANES), F32),
            pltpu.VMEM((2, 2, depth - 1, 6, rows3, LANES), F32),
            pltpu.VMEM((2, 2, 3, width, LANES), F32),
            pltpu.VMEM((2, 2, 2, size // LANES, half, LANES), F32),
            pltpu.VMEM((2, 2, 2, half, LANES), F32),
            pltpu.VMEM((2, 2, 2, half, LANES), F32),
            pltpu.VMEM((4, half // 2, LANES), F32),
            pltpu.VMEM((4, half, LANES), F32),
            pltpu.VMEM((2, 2, half, LANES), F32),
            pltpu.VMEM((2, 2, half, LANES), F32),
            pltpu.VMEM((4, half // 2, LANES), F32),
            pltpu.VMEM((2, 2, tile, LANES), F32),
            pltpu.VMEM((2, 2, tile, LANES), F32),
            pltpu.VMEM((2, 8, LANES), F32),
            pltpu.VMEM((2, 8, LANES), F32),
            pltpu.VMEM((2, 8, LANES), F32),
            pltpu.VMEM((2, depth * cols - 1, 8, LANES), F32),
            pltpu.VMEM((3, width // LANES, width, LANES), F32),
            pltpu.VMEM((3, width, width), F32),
            pltpu.SemaphoreType.DMA((8,)),
            pltpu.SemaphoreType.DMA((semaphores,)),
            pltpu.SemaphoreType.DMA((semaphores,)),
        ],
        compiler_params=pltpu.CompilerParams(
            collective_id=0, has_side_effects=True, vmem_limit_bytes=60 * 1024 * 1024
        ),
        name="refine",
    )(object_field, probe, coeffs, patterns, jnp.swapaxes(offsets, 2, 3), left, right)
    return close(*refined)


def close_kernel(field, coeffs, field_out, coeffs_out, held, sems):
    planes = [(field.at[i], field_out.at[i]) for i in range(field.shape[0])]
    planes += [(coeffs.at[i], coeffs_out.at[i]) for i in range(coeffs.shape[0])]
    copies = [
        (pltpu.make_async_copy(source, held.at[n], sems.at[0, n]), pltpu.make_async_copy(held.at[n], target, sems.at[1, n]))
        for n, (source, target) in enumerate(planes)
    ]
    for come, _ in copies:
        come.start()
    for come, go in copies:
        come.wait()
        go.start()
    for _, go in copies:
        go.wait()


def close(field, coeffs):
    hbm = pl.BlockSpec(memory_space=pl.ANY)
    count = field.shape[0] + coeffs.shape[0]
    return pl.pallas_call(
        close_kernel,
        out_shape=tuple(jax.ShapeDtypeStruct(a.shape, a.dtype) for a in (field, coeffs)),
        in_specs=[hbm] * 2,
        out_specs=(hbm, hbm),
        scratch_shapes=[pltpu.VMEM((count,) + field.shape[1:], F32), pltpu.SemaphoreType.DMA((2, count))],
        compiler_params=pltpu.CompilerParams(vmem_limit_bytes=60 * 1024 * 1024),
        name="close",
    )(field, coeffs)


def solution(mesh):
    placed = (
        P(None, "row", "col"),
        P(),
        P(),
        P("row", "col", None, None, None),
        P("row", "col", None, None),
    )
    return jax.shard_map(
        local, mesh=mesh, in_specs=placed, out_specs=(P(None, "row", "col"), P()), check_vma=False
    )
```

```python
import functools

import jax
import jax.numpy as jnp
import ml_dtypes
import numpy as np
from jax import lax
from jax.experimental import pallas as pl
from jax.experimental.pallas import tpu as pltpu
from jax.sharding import PartitionSpec as P

STEP_RATE = 0.2
RIDGE = 1.0
EPSILON = 1e-06
LANES = 128
CHUNK = 16
F32 = jnp.float32
BF16 = jnp.bfloat16


def dft_halves(order):
    half = order // 2
    index = np.arange(order)
    angle = -2.0 * np.pi / order * (index[:, None] * index[None, :] % order)
    real, imag = np.cos(angle) / np.sqrt(order), np.sin(angle) / np.sqrt(order)
    lefts, rights = [], []
    for parity in (0, 1):
        re, im = real[parity::2, :half], imag[parity::2, :half]
        full = np.block([[re, -im], [im, re]]).astype(np.float32)
        for into, forward in ((lefts, full), (rights, full.T)):
            high = forward.astype(ml_dtypes.bfloat16)
            low = (forward - high.astype(np.float32)).astype(ml_dtypes.bfloat16)
            into.append((high, low))
    wide = lambda pair: np.concatenate([pair[0], pair[0], pair[1]], axis=1)
    tall = lambda pair: np.concatenate([pair[0], pair[0], pair[1]], axis=0)
    on_left = [wide(m) for m in lefts] + [wide(m) for m in rights]
    on_right = [tall(m) for m in rights] + [tall(m) for m in lefts]
    order_of = np.concatenate([index[0::2], index[1::2]])
    perm = (order_of[:, None] == index[None, :]).astype(ml_dtypes.bfloat16)
    on_left.append(np.concatenate([perm] * 3, axis=1))
    on_right.append(np.concatenate([perm.T] * 3, axis=0))
    on_right.append(np.concatenate([perm] * 3, axis=0))
    return jnp.asarray(np.stack(on_left)), jnp.asarray(np.stack(on_right))


def dot(left, right):
    return jnp.dot(left, right, preferred_element_type=F32)


def split(full):
    high = full.astype(BF16)
    return high, (full - high.astype(F32)).astype(BF16)


def split3(full):
    high = full.astype(BF16)
    rest = full - high.astype(F32)
    mid = rest.astype(BF16)
    return high, mid, (rest - mid.astype(F32)).astype(BF16)


def from_left(matrix, full):
    high, low = split(full)
    return dot(matrix, jnp.concatenate([high, low, high], axis=0))


class Copies:
    def __init__(self, send, recv):
        self.send, self.recv, self.used, self.made, self.ended = send, recv, 0, [], 0

    def make(self, source, target, row=None, col=None, sends=None, gets=None):
        slot = self.used
        self.used += 1
        where = (lax.axis_index("row") if row is None else row, lax.axis_index("col") if col is None else col)
        copy = pltpu.make_async_remote_copy(
            src_ref=source, dst_ref=target, send_sem=self.send.at[slot], recv_sem=self.recv.at[slot],
            device_id=where, device_id_type=pl.DeviceIdType.MESH,
        )
        made = Copy(copy, sends, gets)
        self.made.append(made)
        return made

    def finish(self, mark=None):
        mark = len(self.made) if mark is None else mark
        for made in self.made[self.ended:mark]:
            made.sent()
        self.ended = mark


def when(condition, act):
    if condition is None:
        act()
    else:
        pl.when(condition)(act)


class Copy:
    def __init__(self, copy, sends, gets):
        self.copy, self.sends, self.gets = copy, sends, gets

    def start(self):
        when(self.sends, self.copy.start)
        return self

    def arrived(self):
        when(self.gets, self.copy.wait_recv)

    def sent(self):
        when(self.sends, self.copy.wait_send)


def both(a, b):
    return b if a is None else a if b is None else a & b


def copies_needed(rows, cols):
    return 160 + 4 * (rows + cols) + rows * cols


def refine_kernel(field_hbm, probe_hbm, coeffs_hbm, pats_hbm, offs, left_hbm, right_hbm,
                  field_out, coeffs_out,
                  ext, grads, gext, pads, psi, phi, highs, lows, probe, coeffs, pats, left, right,
                  stats, half_sums, col_sums, shard, z_sums, new_coeffs,
                  folds, got_x, got_g, relay_in, relay_g, last_x, last_g, relay_last, base, gtile,
                  sq_mine, sq_pair, sq_part, sq_all, woven, acc,
                  local_sem, send_sem, recv_sem):
    rows, cols = lax.axis_size("row"), lax.axis_size("col")
    r, c = lax.axis_index("row"), lax.axis_index("col")
    depth = rows // 2
    k, z = lax.rem(r, 2), lax.div(r, 2)
    count = pats.shape[0]
    width = probe.shape[1]
    half = width // 2
    size = ext.shape[2]
    tile = size - width
    top = half + tile
    net = Copies(send_sem, recv_sem)

    partner = r + 1 - 2 * k
    beyond = r - 1 + 2 * k
    has_z = (beyond >= 0) & (beyond < rows)
    beyond = lax.rem(beyond + rows, rows)
    odd_c = lax.rem(c, 2)
    step_g = 2 * odd_c - 1
    has_g = (c + step_g >= 0) & (c + step_g < cols)
    has_r = (c - 2 * step_g >= 0) & (c - 2 * step_g < cols)
    col_x = c - step_g
    col_g = lax.rem(c + step_g + cols, cols)
    col_r = lax.rem(c + 2 * step_g + 2 * cols, cols)

    def chip(dz, dc):
        return 2 * lax.rem(z + dz, depth) + k, lax.rem(c + dc, cols)

    others = [(dz, dc) for dz in range(depth) for dc in range(cols) if dz or dc]

    barrier = pltpu.get_barrier_semaphore()

    def greet(row, col):
        pl.semaphore_signal(barrier, inc=1, device_id=(row, col), device_id_type=pl.DeviceIdType.MESH)

    for dz, dc in others:
        greet(*chip(dz, dc))
    greet(partner, c)
    when(has_z, lambda: greet(beyond, c))
    greeted = len(others) + 1 + has_z.astype(jnp.int32)

    inner = pl.ds(half, tile)
    loads = []

    def load(source, target):
        copy = pltpu.make_async_copy(source, target, local_sem.at[len(loads)])
        copy.start()
        loads.append(copy)
        return copy

    field_loads = [
        load(field_hbm.at[:, :, pl.ds(b * LANES, LANES)], ext.at[:, 1 + b, inner, :]) for b in (0, 1)
    ]
    pats_load = load(pats_hbm.at[0, 0], pats)
    coeffs_load = load(coeffs_hbm, acc)
    left_load = load(left_hbm, left)
    right_load = load(right_hbm, right)
    probe_load = load(probe_hbm, probe)

    for edge, b in ((c == 0, 0), (c == cols - 1, 3)):
        @pl.when(edge)
        def _():
            ext[:, b] = jnp.zeros((2, size, LANES), F32)
            gext[:, b] = jnp.zeros((2, size, LANES), F32)
    for edge, start in ((r == 0, 0), (r == rows - 1, top)):
        @pl.when(edge)
        def _():
            ext[:, :, pl.ds(start, half), :] = jnp.zeros((2, 4, half, LANES), F32)
            gext[:, :, pl.ds(start, half), :] = jnp.zeros((2, 4, half, LANES), F32)

    def clear(p, carry):
        for part in (0, 1):
            for b in (0, 4):
                pads[p, part, b] = jnp.zeros((3 * width, LANES), F32)
            for b in (1, 2, 3):
                for start in (0, 2 * width):
                    pads[p, part, b, pl.ds(start, width), :] = jnp.zeros((width, LANES), F32)
        return carry

    lax.fori_loop(0, count, clear, 0)
    for copy in field_loads:
        copy.wait()
    pl.semaphore_wait(barrier, greeted)

    def rows_of(which):
        return half * (1 - k) if which == 0 else half * k

    def side_row(which):
        return top * k if which == 0 else top * (1 - k)

    def edge_row(which):
        return top * (1 - k) if which == 0 else top * k

    def at(start, length):
        return pl.ds(pl.multiple_of(start, 8), length)

    side_dev = (partner, beyond)
    side_has = (None, has_z)

    ends = []
    for which in (1, 0):
        mine = at(half + rows_of(which), half)
        there = at(side_row(which), half)
        ends.append(net.make(ext.at[:, pl.ds(1, 2), mine, :], ext.at[:, pl.ds(1, 2), there, :],
                             row=side_dev[which], sends=side_has[which], gets=side_has[which]).start())

    edge_x, edge_g = 2 - odd_c, 1 + odd_c
    out_x, out_g = 3 * (1 - odd_c), 3 * odd_c
    far_x, far_g = 3 * odd_c, 3 * (1 - odd_c)
    quarter = half // 2
    first_units = [(1, 0), (1, 1), (0, 0), (0, 1)]

    def exchange(units, sources, targets, relays):
        made = {}
        for n, unit in enumerate(units):
            sx, sg1, sg2 = sources(*unit)
            tx, tg1, tg2 = targets(*unit)
            made[unit] = (
                net.make(sx, tx, col=col_x),
                net.make(sg1, tg1, col=col_g, sends=has_g, gets=has_g),
                net.make(sg2, relays.at[n], col=col_r, sends=has_g, gets=has_r),
                net.make(relays.at[n], tg2, col=col_x, sends=has_r, gets=has_g),
            )
        return made

    def push(copies):
        copies[2].start()
        copies[0].start()
        copies[1].start()

    def hand_on(copies):
        copies[2].arrived()
        copies[3].start()

    def first_sources(which, part):
        start = half + rows_of(which)
        return (ext.at[part, edge_x, at(start, half), :],
                ext.at[part, edge_g, at(start, quarter), :],
                ext.at[part, edge_g, at(start + quarter, quarter), :])

    def first_targets(which, part):
        start = half + rows_of(which)
        return (ext.at[part, far_x, at(start, half), :],
                ext.at[part, far_g, at(start, quarter), :],
                ext.at[part, far_g, at(start + quarter, quarter), :])

    side = exchange(first_units, first_sources, first_targets, relay_in)
    def straight(unit):
        side[unit][0].start()
        side[unit][1].start()

    for unit in first_units:
        side[unit][2].start()
    for unit in first_units[:3]:
        straight(unit)

    def reorder(full):
        part = dot(jnp.concatenate(split3(full), axis=1), right[4])
        return dot(left[4], jnp.concatenate(split3(part), axis=0))

    def reorder_pats(p, carry):
        pats[p] = reorder(pats[p])
        return carry

    for copy in (pats_load, left_load, right_load, coeffs_load, probe_load):
        copy.wait()
    lax.fori_loop(0, count // 2, reorder_pats, 0)
    hand_on(side[first_units[0]])
    hand_on(side[first_units[1]])
    straight(first_units[3])
    lax.fori_loop(count // 2, count, reorder_pats, 0)
    hand_on(side[first_units[2]])
    hand_on(side[first_units[3]])
    for i in range(3):
        full = reorder(acc[i])
        for parity in (0, 1):
            coeffs[parity, i] = full[:, parity * LANES:(parity + 1) * LANES]

    corners = []

    def corner(unit, arrivals, b, has):
        which, part = unit
        for i in arrivals:
            side[unit][i].arrived()
        cond = both(has, side_has[which])
        mine = at(half + rows_of(which), half)
        there = at(side_row(which), half)
        corners.append(net.make(ext.at[part, b, mine, :], ext.at[part, b, there, :],
                                row=side_dev[which], sends=cond, gets=cond).start())

    for pair in (first_units[:2], first_units[2:]):
        for unit in pair:
            corner(unit, (0,), out_x, None)
        for unit in pair:
            corner(unit, (1, 3), out_g, has_g)
    for copy in ends + corners:
        copy.arrived()

    lane = lax.broadcasted_iota(jnp.int32, (1, LANES), 1)

    def place(p):
        oy, ox = offs[0, 0, 0, p], offs[0, 0, 1, p]
        block = lax.div(ox, LANES)
        return oy, block, ox - block * LANES

    def forward(source):
        def visit(p, carry):
            oy, block, shift = place(p)
            window = []
            keep = lane < LANES - shift
            for part in (0, 1):
                turned = [
                    pltpu.roll(source[part, block + j, pl.ds(oy, width), :], lax.rem(LANES - shift, LANES), axis=1)
                    for j in range(3)
                ]
                window.append([jnp.where(keep, turned[j], turned[j + 1]) for j in (0, 1)])
            sums, difs = [[], []], [[], []]
            for h in (0, 1):
                pr, pi = probe[0, :, h * LANES:(h + 1) * LANES], probe[1, :, h * LANES:(h + 1) * LANES]
                wr, wi = window[0][h], window[1][h]
                for part, x in ((0, pr * wr - pi * wi), (1, pr * wi + pi * wr)):
                    sums[part].append(x[:half] + x[half:])
                    difs[part].append(x[:half] - x[half:])
            bands = []
            for parity, group in ((0, sums), (1, difs)):
                stack = jnp.concatenate([jnp.concatenate(group[part], axis=1) for part in (0, 1)], axis=0)
                bands.append(from_left(left[parity], stack))
            re = jnp.concatenate([bands[0][:half], bands[1][:half]], axis=0)
            im = jnp.concatenate([bands[0][half:], bands[1][half:]], axis=0)
            plus = jnp.concatenate([re[:, :half] + re[:, half:], im[:, :half] + im[:, half:]], axis=1)
            minus = jnp.concatenate([re[:, :half] - re[:, half:], im[:, :half] - im[:, half:]], axis=1)
            for parity, full in ((0, plus), (1, minus)):
                highs[p, parity], lows[p, parity] = split(full)
            return carry

        lax.fori_loop(0, count, visit, 0, unroll=True)

    def finish_forward(parity, into):
        def visit(p, carry):
            high, low = highs[p, parity], lows[p, parity]
            into[p, parity] = dot(jnp.concatenate([high, low, high], axis=1), right[parity])
            return carry

        lax.fori_loop(0, count, visit, 0, unroll=True)

    def detect(turn, parity, response, rate):
        span = slice(parity * LANES, (parity + 1) * LANES)

        def chunk(i, carry):
            here = pl.ds(pl.multiple_of(i * CHUNK, CHUNK), CHUNK)
            lin, quad, cubic = (response[parity, j, here, :] for j in range(3))
            sums = [jnp.zeros((CHUNK, LANES), F32)] * 6
            for p in range(count):
                wr, wi = psi[p, parity, here, :LANES], psi[p, parity, here, LANES:]
                if rate is not None:
                    wr -= rate * phi[p, parity, here, :LANES]
                    wi -= rate * phi[p, parity, here, LANES:]
                inten = wr * wr + wi * wi
                error = inten * (lin + inten * (quad + inten * cubic)) - pats[p, here, span]
                weight = 2.0 * error * (lin + inten * (2.0 * quad + 3.0 * cubic * inten))
                squared = inten * inten
                cubed = squared * inten
                terms = (error * inten, error * squared, error * cubed,
                         squared, squared * squared, cubed * cubed)
                sums = [a + b for a, b in zip(sums, terms)]
                for j, part in ((0, weight * wr), (1, weight * wi)):
                    high, low = split(part)
                    highs[p, parity, here, j * LANES:(j + 1) * LANES] = high
                    lows[p, parity, here, j * LANES:(j + 1) * LANES] = low
            for j in range(6):
                stats[turn, parity, j, here, :] = sums[j]
            return carry

        lax.fori_loop(0, width // CHUNK, chunk, 0, unroll=2)

    def backward():
        def visit(p, carry):
            _, _, shift = place(p)
            bands = []
            for parity in (0, 1):
                high, low = highs[p, parity], lows[p, parity]
                bands.append(dot(jnp.concatenate([high, low, high], axis=1), right[2 + parity]))
            plus, minus = bands[0] + bands[1], bands[0] - bands[1]
            re = jnp.concatenate([plus[:, :half], minus[:, :half]], axis=1)
            im = jnp.concatenate([plus[:, half:], minus[:, half:]], axis=1)
            bands = []
            for parity in (0, 1):
                rows_in = slice(parity * half, (parity + 1) * half)
                bands.append(from_left(left[2 + parity], jnp.concatenate([re[rows_in], im[rows_in]], axis=0)))
            plus, minus = bands[0] + bands[1], bands[0] - bands[1]
            xr = jnp.concatenate([plus[:half], minus[:half]], axis=0)
            xi = jnp.concatenate([plus[half:], minus[half:]], axis=0)
            pr, pi = probe[0], probe[1]
            keep = lane >= shift
            for part, g in ((0, pr * xr + pi * xi), (1, pr * xi - pi * xr)):
                a = pltpu.roll(g[:, :LANES], shift, axis=1)
                b = pltpu.roll(g[:, LANES:], shift, axis=1)
                zero = jnp.zeros_like(a)
                pads[p, part, 1, pl.ds(width, width), :] = jnp.where(keep, a, zero)
                pads[p, part, 2, pl.ds(width, width), :] = jnp.where(keep, b, a)
                pads[p, part, 3, pl.ds(width, width), :] = jnp.where(keep, zero, b)
            return carry

        lax.fori_loop(0, count, visit, 0, unroll=True)

    def gather(turn, start, length):
        for part in (0, 1):
            for b in range(4):
                total = 0.0
                for p in range(count):
                    oy, block, _ = place(p)
                    total += pads[p, part, b + 1 - block, pl.ds(width - oy + start, length), :]
                grads[turn, part, b, pl.ds(start, length), :] = total

    rows1 = width // 2
    rows2, rows3 = shard.shape[3], z_sums.shape[4]
    cut = rows3 < rows2

    class Sums:
        def __init__(self, turn, parity, old):
            self.at, self.old = (turn, parity), old
            self.base2 = k * rows1 + c * rows2
            self.base3 = self.base2 + z * rows3 if cut else self.base2

        def pair(self):
            t = self.at
            self.first = net.make(stats.at[*t, :, at((1 - k) * rows1, rows1), :], half_sums.at[t], row=partner).start()

        def over_cols(self):
            t = self.at
            self.first.arrived()
            half_sums[t] += stats[*t, :, at(k * rows1, rows1), :]
            self.copies = []
            for d in range(1, cols):
                other = lax.rem(c + d, cols)
                self.copies.append(net.make(half_sums.at[*t, :, at(other * rows2, rows2), :],
                                            col_sums.at[*t, d - 1], col=other).start())

        def over_z(self):
            t = self.at
            for copy in self.copies:
                copy.arrived()
            shard[t] = half_sums[*t, :, at(c * rows2, rows2), :] + sum(col_sums[*t, d] for d in range(cols - 1))
            self.copies = []
            for d in range(1, depth):
                other = lax.rem(z + d, depth)
                source = shard.at[*t, :, at(other * rows3, rows3), :] if cut else shard.at[t]
                self.copies.append(net.make(source, z_sums.at[*t, d - 1], row=2 * other + k).start())

        def update(self):
            t = self.at
            for copy in self.copies:
                copy.arrived()
            own = shard[*t, :, at(z * rows3, rows3), :] if cut else shard[t]
            sums = own + sum(z_sums[*t, i] for i in range(depth - 1))
            new_coeffs[*t, :, at(self.base3, rows3), :] = (
                self.old[t[1], :, at(self.base3, rows3), :] - sums[:3] / (sums[3:] + RIDGE))
            self.copies = []
            if cut:
                ready = new_coeffs.at[*t, :, at(self.base3, rows3), :]
                for d in range(1, depth):
                    self.copies.append(net.make(ready, ready, row=2 * lax.rem(z + d, depth) + k).start())

        def spread(self):
            for copy in self.copies:
                copy.arrived()
            ready = new_coeffs.at[*self.at, :, at(self.base2, rows2), :]
            self.copies = [net.make(ready, ready, col=lax.rem(c + d, cols)).start() for d in range(1, cols)]

        def swap(self):
            for copy in self.copies:
                copy.arrived()
            ready = new_coeffs.at[*self.at, :, at(k * rows1, rows1), :]
            self.end = net.make(ready, ready, row=partner).start()

        def done(self):
            self.end.arrived()

    class Norm:
        def __init__(self, turn):
            self.turn = turn

        def pair(self, square):
            t = self.turn
            sq_mine[t] = square
            self.first = net.make(sq_mine.at[t], sq_pair.at[t], row=partner).start()

        def wide(self):
            t = self.turn
            self.first.arrived()
            sq_part[t] = sq_mine[t] + sq_pair[t]
            self.copies = []
            for i, place in enumerate(others):
                row, col = chip(*place)
                self.copies.append(net.make(sq_part.at[t], sq_all.at[t, i], row=row, col=col).start())

        def rate(self):
            t = self.turn
            for copy in self.copies:
                copy.arrived()
            square = sq_part[t] + sum(sq_all[t, i] for i in range(len(others)))
            total = 2.0 * tile * tile * rows * cols
            return STEP_RATE / jnp.sqrt(jnp.sum(square, keepdims=True) / total + EPSILON)

    def fold_rows(turn):
        made = {}
        for which in (1, 0):
            for part in (0, 1):
                made[(which, part)] = net.make(
                    grads.at[turn, part, :, at(edge_row(which), half), :], folds.at[turn, which, part],
                    row=side_dev[which], sends=side_has[which], gets=side_has[which],
                ).start()
        return made

    def add_fold(turn, made, which, part):
        made[(which, part)].arrived()

        def add():
            grads[turn, part, :, at(half + rows_of(which), half), :] += folds[turn, which, part]

        when(side_has[which], add)

    block_x, block_g = 2 * (1 - odd_c), 2 * odd_c

    forward(ext)
    sums0 = [Sums(0, parity, coeffs) for parity in (0, 1)]
    finish_forward(0, psi)
    detect(0, 0, coeffs, None)
    sums0[0].pair()
    finish_forward(1, psi)
    detect(0, 1, coeffs, None)
    sums0[1].pair()
    sums0[0].over_cols()
    backward()
    sums0[1].over_cols()
    gather(0, 0, half)
    gather(0, top, half)
    made = fold_rows(0)
    gather(0, half, tile)

    units = [(0, 0), (1, 0), (1, 1), (0, 1)]

    def mid_sources(which, part):
        here = at(half + rows_of(which), half)
        return (grads.at[0, part, pl.ds(block_x, 2), here, :],
                grads.at[0, part, block_g, here, :],
                grads.at[0, part, block_g + 1, here, :])

    def mid_targets(which, part):
        return got_x.at[which, part], got_g.at[which, part, 0], got_g.at[which, part, 1]

    mids = exchange(units, mid_sources, mid_targets, relay_g)
    sides = []

    def take(unit):
        which, part = unit
        here = at(half + rows_of(which), half)
        mids[unit][0].arrived()
        gext[part, pl.ds(block_x, 2), here, :] = grads[0, part, pl.ds(block_x, 2), here, :] + got_x[which, part]
        mids[unit][1].arrived()
        mids[unit][3].arrived()

        @pl.when(has_g)
        def _():
            gext[part, pl.ds(block_g, 2), here, :] = grads[0, part, pl.ds(block_g, 2), here, :] + got_g[which, part]

        @pl.when(jnp.logical_not(has_g))
        def _():
            gext[part, edge_g, here, :] = grads[0, part, edge_g, here, :]

        sides.append(net.make(
            gext.at[part, :, here, :], gext.at[part, :, at(side_row(which), half), :],
            row=side_dev[which], sends=side_has[which], gets=side_has[which],
        ).start())

    add_fold(0, made, *units[0])
    push(mids[units[0]])
    sums0[0].over_z()
    add_fold(0, made, *units[1])
    push(mids[units[1]])
    hand_on(mids[units[0]])
    for unit in units[2:]:
        add_fold(0, made, *unit)
        push(mids[unit])
    sums0[0].update()
    sums0[1].over_z()
    for unit in units[1:]:
        hand_on(mids[unit])
    take(units[0])
    sums0[0].spread()
    sums0[1].update()
    take(units[1])
    take(units[2])
    sums0[1].spread()
    take(units[3])

    def squares(blocks):
        total = 0.0
        for block in blocks:
            total += jnp.sum((block * block).reshape(-1, 8, LANES), axis=0)
        return total

    norm0 = Norm(0)
    mark = len(net.made)
    norm0.pair(squares([gext[part, b, inner, :] for part in (0, 1) for b in (1, 2)]))
    for copy in sides:
        copy.arrived()
    norm0.wide()

    sums0[0].swap()
    forward(gext)
    sums0[1].swap()
    finish_forward(0, phi)
    net.finish(mark)
    rate0 = norm0.rate()
    sums0[0].done()
    sums1 = [Sums(1, parity, new_coeffs.at[0]) for parity in (0, 1)]
    detect(1, 0, new_coeffs.at[0], rate0)
    sums1[0].pair()
    finish_forward(1, phi)
    sums0[1].done()
    detect(1, 1, new_coeffs.at[0], rate0)
    sums1[1].pair()
    sums1[0].over_cols()
    backward()
    sums1[1].over_cols()
    gather(1, 0, half)
    gather(1, top, half)
    made = fold_rows(1)
    gather(1, half, tile)

    units = [(0, 0), (0, 1), (1, 0), (1, 1)]

    def last_sources(which, part):
        start = half + rows_of(which)
        return (grads.at[1, part, out_x, at(start, half), :],
                grads.at[1, part, out_g, at(start, quarter), :],
                grads.at[1, part, out_g, at(start + quarter, quarter), :])

    def last_targets(which, part):
        return (last_x.at[which, part], last_g.at[which, part, pl.ds(0, quarter), :],
                last_g.at[which, part, pl.ds(quarter, quarter), :])

    lasts = exchange(units, last_sources, last_targets, relay_last)
    for part in (0, 1):
        for b in (0, 1):
            base[part, b] = ext[part, 1 + b, inner, :] - rate0 * gext[part, 1 + b, inner, :]
    def settle(unit):
        which, part = unit
        here = at(half + rows_of(which), half)
        there = at(rows_of(which), half)
        lasts[(which, part)][0].arrived()
        lasts[(which, part)][1].arrived()
        lasts[(which, part)][3].arrived()
        mine = grads[1, part, edge_x, here, :] + last_x[which, part]
        gtile[part, edge_x - 1, there, :] = mine
        square = squares([mine])

        @pl.when(has_g)
        def _():
            gtile[part, edge_g - 1, there, :] = grads[1, part, edge_g, here, :] + last_g[which, part]

        @pl.when(jnp.logical_not(has_g))
        def _():
            gtile[part, edge_g - 1, there, :] = grads[1, part, edge_g, here, :]

        return square + squares([gtile[part, edge_g - 1, there, :]])

    for unit in units[:2]:
        add_fold(1, made, *unit)
        push(lasts[unit])
    sums1[0].over_z()
    add_fold(1, made, *units[2])
    push(lasts[units[2]])
    hand_on(lasts[units[0]])
    hand_on(lasts[units[1]])
    sums1[0].update()
    add_fold(1, made, *units[3])
    push(lasts[units[3]])
    sums1[1].over_z()
    hand_on(lasts[units[2]])
    mark = len(net.made)
    sums1[0].spread()
    hand_on(lasts[units[3]])
    sums1[1].update()
    square = 0.0
    for unit in units:
        square += settle(unit)
    norm1 = Norm(1)
    norm1.pair(square)
    sums1[1].spread()
    norm1.wide()
    sums1[0].swap()
    net.finish(mark)
    rate1 = norm1.rate()
    for part in (0, 1):
        for b in (0, 1):
            field_out[part, :, b * LANES:(b + 1) * LANES] = base[part, b] - rate1 * gtile[part, b]
    sums1[0].done()

    def natural(i, parity):
        begin = parity * LANES
        spread = jnp.concatenate([right[5, j * width + begin:j * width + begin + LANES, :] for j in range(3)], axis=0)
        return dot(jnp.concatenate(split3(new_coeffs[1, parity, i]), axis=1), spread)

    for i in range(3):
        acc[i] = natural(i, 0)
    sums1[1].swap()
    sums1[1].done()
    for i in range(3):
        full = acc[i] + natural(i, 1)
        for b in (0, 1):
            span = slice(b * LANES, (b + 1) * LANES)
            for parity in (0, 1):
                woven[i, b, pl.ds(parity, half, stride=2), :] = full[parity * half:(parity + 1) * half, span]
            coeffs_out[i, :, span] = woven[i, b]
    net.finish()


def local(object_field, probe, coeffs, patterns, offsets):
    rows, cols = lax.axis_size("row"), lax.axis_size("col")
    depth = rows // 2
    count, width = patterns.shape[2], probe.shape[1]
    half = width // 2
    tile = object_field.shape[1]
    size = tile + width
    rows1 = width // 2
    rows2 = rows1 // cols
    rows3 = rows2 // depth if rows2 % (8 * depth) == 0 else rows2
    left, right = dft_halves(width)
    vmem = pl.BlockSpec(memory_space=pltpu.VMEM)
    hbm = pl.BlockSpec(memory_space=pltpu.HBM)
    semaphores = copies_needed(rows, cols)
    extended = (2, size // LANES, size, LANES)
    freq = (count, 2, width, width)
    refined = pl.pallas_call(
        refine_kernel,
        out_shape=(
            jax.ShapeDtypeStruct((2, tile, tile), F32),
            jax.ShapeDtypeStruct(coeffs.shape, F32),
        ),
        in_specs=[hbm] * 4 + [pl.BlockSpec(memory_space=pltpu.SMEM)] + [hbm] * 2,
        out_specs=(vmem, vmem),
        scratch_shapes=[
            pltpu.VMEM(extended, F32),
            pltpu.VMEM((2,) + extended, F32),
            pltpu.VMEM(extended, F32),
            pltpu.VMEM((count, 2, 5, 3 * width, LANES), F32),
            pltpu.VMEM(freq, F32),
            pltpu.VMEM(freq, F32),
            pltpu.VMEM(freq, BF16),
            pltpu.VMEM(freq, BF16),
            pltpu.VMEM((2, width, width), F32),
            pltpu.VMEM((2, 3, width, LANES), F32),
            pltpu.VMEM((count, width, width), F32),
            pltpu.VMEM(left.shape, BF16),
            pltpu.VMEM(right.shape, BF16),
            pltpu.VMEM((2, 2, 6, width, LANES), F32),
            pltpu.VMEM((2, 2, 6, rows1, LANES), F32),
            pltpu.VMEM((2, 2, cols - 1, 6, rows2, LANES), F32),
            pltpu.VMEM((2, 2, 6, rows2, LANES), F32),
            pltpu.VMEM((2, 2, depth - 1, 6, rows3, LANES), F32),
            pltpu.VMEM((2, 2, 3, width, LANES), F32),
            pltpu.VMEM((2, 2, 2, size // LANES, half, LANES), F32),
            pltpu.VMEM((2, 2, 2, half, LANES), F32),
            pltpu.VMEM((2, 2, 2, half, LANES), F32),
            pltpu.VMEM((4, half // 2, LANES), F32),
            pltpu.VMEM((4, half, LANES), F32),
            pltpu.VMEM((2, 2, half, LANES), F32),
            pltpu.VMEM((2, 2, half, LANES), F32),
            pltpu.VMEM((4, half // 2, LANES), F32),
            pltpu.VMEM((2, 2, tile, LANES), F32),
            pltpu.VMEM((2, 2, tile, LANES), F32),
            pltpu.VMEM((2, 8, LANES), F32),
            pltpu.VMEM((2, 8, LANES), F32),
            pltpu.VMEM((2, 8, LANES), F32),
            pltpu.VMEM((2, depth * cols - 1, 8, LANES), F32),
            pltpu.VMEM((3, width // LANES, width, LANES), F32),
            pltpu.VMEM((3, width, width), F32),
            pltpu.SemaphoreType.DMA((8,)),
            pltpu.SemaphoreType.DMA((semaphores,)),
            pltpu.SemaphoreType.DMA((semaphores,)),
        ],
        compiler_params=pltpu.CompilerParams(
            collective_id=0, has_side_effects=True, vmem_limit_bytes=60 * 1024 * 1024
        ),
        name="refine",
    )(object_field, probe, coeffs, patterns, jnp.swapaxes(offsets, 2, 3), left, right)
    return close(*refined)


def close_kernel(field, coeffs, field_out, coeffs_out, held, sems):
    planes = [(field.at[i], field_out.at[i]) for i in range(field.shape[0])]
    planes += [(coeffs.at[i], coeffs_out.at[i]) for i in range(coeffs.shape[0])]
    copies = [
        (pltpu.make_async_copy(source, held.at[n], sems.at[0, n]), pltpu.make_async_copy(held.at[n], target, sems.at[1, n]))
        for n, (source, target) in enumerate(planes)
    ]
    for come, _ in copies:
        come.start()
    for come, go in copies:
        come.wait()
        go.start()
    for _, go in copies:
        go.wait()


def close(field, coeffs):
    hbm = pl.BlockSpec(memory_space=pl.ANY)
    count = field.shape[0] + coeffs.shape[0]
    return pl.pallas_call(
        close_kernel,
        out_shape=tuple(jax.ShapeDtypeStruct(a.shape, a.dtype) for a in (field, coeffs)),
        in_specs=[hbm] * 2,
        out_specs=(hbm, hbm),
        scratch_shapes=[pltpu.VMEM((count,) + field.shape[1:], F32), pltpu.SemaphoreType.DMA((2, count))],
        compiler_params=pltpu.CompilerParams(vmem_limit_bytes=60 * 1024 * 1024),
        name="close",
    )(field, coeffs)


def solution(mesh):
    placed = (
        P(None, "row", "col"),
        P(),
        P(),
        P("row", "col", None, None, None),
        P("row", "col", None, None),
    )
    return jax.shard_map(
        local, mesh=mesh, in_specs=placed, out_specs=(P(None, "row", "col"), P()), check_vma=False
    )
```

```python
import functools

import jax
import jax.numpy as jnp
import ml_dtypes
import numpy as np
from jax import lax
from jax.experimental import pallas as pl
from jax.experimental.pallas import tpu as pltpu
from jax.sharding import PartitionSpec as P

STEP_RATE = 0.2
RIDGE = 1.0
EPSILON = 1e-06
LANES = 128
CHUNK = 16
F32 = jnp.float32
BF16 = jnp.bfloat16


def dft_halves(order):
    half = order // 2
    index = np.arange(order)
    angle = -2.0 * np.pi / order * (index[:, None] * index[None, :] % order)
    real, imag = np.cos(angle) / np.sqrt(order), np.sin(angle) / np.sqrt(order)
    lefts, rights = [], []
    for parity in (0, 1):
        re, im = real[parity::2, :half], imag[parity::2, :half]
        full = np.block([[re, -im], [im, re]]).astype(np.float32)
        for into, forward in ((lefts, full), (rights, full.T)):
            high = forward.astype(ml_dtypes.bfloat16)
            low = (forward - high.astype(np.float32)).astype(ml_dtypes.bfloat16)
            into.append((high, low))
    wide = lambda pair: np.concatenate([pair[0], pair[0], pair[1]], axis=1)
    tall = lambda pair: np.concatenate([pair[0], pair[0], pair[1]], axis=0)
    on_left = [wide(m) for m in lefts] + [wide(m) for m in rights]
    on_right = [tall(m) for m in rights] + [tall(m) for m in lefts]
    order_of = np.concatenate([index[0::2], index[1::2]])
    perm = (order_of[:, None] == index[None, :]).astype(ml_dtypes.bfloat16)
    on_left.append(np.concatenate([perm] * 3, axis=1))
    on_right.append(np.concatenate([perm.T] * 3, axis=0))
    on_right.append(np.concatenate([perm] * 3, axis=0))
    return jnp.asarray(np.stack(on_left)), jnp.asarray(np.stack(on_right))


def dot(left, right):
    return jnp.dot(left, right, preferred_element_type=F32)


def split(full):
    high = full.astype(BF16)
    return high, (full - high.astype(F32)).astype(BF16)


def split3(full):
    high = full.astype(BF16)
    rest = full - high.astype(F32)
    mid = rest.astype(BF16)
    return high, mid, (rest - mid.astype(F32)).astype(BF16)


def from_left(matrix, full):
    high, low = split(full)
    return dot(matrix, jnp.concatenate([high, low, high], axis=0))


class Copies:
    def __init__(self, send, recv):
        self.send, self.recv, self.used, self.made, self.ended = send, recv, 0, [], 0

    def make(self, source, target, row=None, col=None, sends=None, gets=None):
        slot = self.used
        self.used += 1
        where = (lax.axis_index("row") if row is None else row, lax.axis_index("col") if col is None else col)
        copy = pltpu.make_async_remote_copy(
            src_ref=source, dst_ref=target, send_sem=self.send.at[slot], recv_sem=self.recv.at[slot],
            device_id=where, device_id_type=pl.DeviceIdType.MESH,
        )
        made = Copy(copy, sends, gets)
        self.made.append(made)
        return made

    def finish(self, mark=None):
        mark = len(self.made) if mark is None else mark
        for made in self.made[self.ended:mark]:
            made.sent()
        self.ended = mark


def when(condition, act):
    if condition is None:
        act()
    else:
        pl.when(condition)(act)


class Copy:
    def __init__(self, copy, sends, gets):
        self.copy, self.sends, self.gets = copy, sends, gets

    def start(self):
        when(self.sends, self.copy.start)
        return self

    def arrived(self):
        when(self.gets, self.copy.wait_recv)

    def sent(self):
        when(self.sends, self.copy.wait_send)


def both(a, b):
    return b if a is None else a if b is None else a & b


def copies_needed(rows, cols):
    return 160 + 4 * (rows + cols) + rows * cols


def refine_kernel(field_hbm, probe_hbm, coeffs_hbm, pats_hbm, offs, left_hbm, right_hbm,
                  field_out, coeffs_out,
                  ext, grads, gext, pads, psi, phi, highs, lows, probe, coeffs, pats, left, right,
                  stats, half_sums, col_sums, shard, z_sums, new_coeffs,
                  folds, got_x, got_g, relay_in, relay_g, last_x, last_g, relay_last, base, gtile,
                  sq_mine, sq_pair, sq_part, sq_all, woven, acc,
                  local_sem, send_sem, recv_sem):
    rows, cols = lax.axis_size("row"), lax.axis_size("col")
    r, c = lax.axis_index("row"), lax.axis_index("col")
    depth = rows // 2
    k, z = lax.rem(r, 2), lax.div(r, 2)
    count = pats.shape[0]
    width = probe.shape[1]
    half = width // 2
    size = ext.shape[2]
    tile = size - width
    top = half + tile
    net = Copies(send_sem, recv_sem)

    partner = r + 1 - 2 * k
    beyond = r - 1 + 2 * k
    has_z = (beyond >= 0) & (beyond < rows)
    beyond = lax.rem(beyond + rows, rows)
    odd_c = lax.rem(c, 2)
    step_g = 2 * odd_c - 1
    has_g = (c + step_g >= 0) & (c + step_g < cols)
    has_r = (c - 2 * step_g >= 0) & (c - 2 * step_g < cols)
    col_x = c - step_g
    col_g = lax.rem(c + step_g + cols, cols)
    col_r = lax.rem(c + 2 * step_g + 2 * cols, cols)

    def chip(dz, dc):
        return 2 * lax.rem(z + dz, depth) + k, lax.rem(c + dc, cols)

    others = [(dz, dc) for dz in range(depth) for dc in range(cols) if dz or dc]

    barrier = pltpu.get_barrier_semaphore()

    def greet(row, col):
        pl.semaphore_signal(barrier, inc=1, device_id=(row, col), device_id_type=pl.DeviceIdType.MESH)

    near = [(0, dc) for dc in range(1, cols)] + [(dz, 0) for dz in range(1, depth)]
    when(has_z, lambda: greet(beyond, c))
    greet(partner, c)
    for dz, dc in near:
        greet(*chip(dz, dc))
    greeted = len(near) + 1 + has_z.astype(jnp.int32)

    inner = pl.ds(half, tile)
    loads = []

    def load(source, target):
        copy = pltpu.make_async_copy(source, target, local_sem.at[len(loads)])
        copy.start()
        loads.append(copy)
        return copy

    field_loads = [
        load(field_hbm.at[:, :, pl.ds(b * LANES, LANES)], ext.at[:, 1 + b, inner, :]) for b in (0, 1)
    ]
    pats_load = load(pats_hbm.at[0, 0], pats)
    coeffs_load = load(coeffs_hbm, acc)
    left_load = load(left_hbm, left)
    right_load = load(right_hbm, right)
    probe_load = load(probe_hbm, probe)

    for edge, b in ((c == 0, 0), (c == cols - 1, 3)):
        @pl.when(edge)
        def _():
            ext[:, b] = jnp.zeros((2, size, LANES), F32)
            gext[:, b] = jnp.zeros((2, size, LANES), F32)
    for edge, start in ((r == 0, 0), (r == rows - 1, top)):
        @pl.when(edge)
        def _():
            ext[:, :, pl.ds(start, half), :] = jnp.zeros((2, 4, half, LANES), F32)
            gext[:, :, pl.ds(start, half), :] = jnp.zeros((2, 4, half, LANES), F32)

    def clear(p, carry):
        for part in (0, 1):
            for b in (0, 4):
                pads[p, part, b] = jnp.zeros((3 * width, LANES), F32)
            for b in (1, 2, 3):
                for start in (0, 2 * width):
                    pads[p, part, b, pl.ds(start, width), :] = jnp.zeros((width, LANES), F32)
        return carry

    lax.fori_loop(0, count, clear, 0)
    for copy in field_loads:
        copy.wait()
    pl.semaphore_wait(barrier, greeted)

    def rows_of(which):
        return half * (1 - k) if which == 0 else half * k

    def side_row(which):
        return top * k if which == 0 else top * (1 - k)

    def edge_row(which):
        return top * (1 - k) if which == 0 else top * k

    def at(start, length):
        return pl.ds(pl.multiple_of(start, 8), length)

    side_dev = (partner, beyond)
    side_has = (None, has_z)

    ends = []
    for which in (1, 0):
        mine = at(half + rows_of(which), half)
        there = at(side_row(which), half)
        ends.append(net.make(ext.at[:, pl.ds(1, 2), mine, :], ext.at[:, pl.ds(1, 2), there, :],
                             row=side_dev[which], sends=side_has[which], gets=side_has[which]).start())

    edge_x, edge_g = 2 - odd_c, 1 + odd_c
    out_x, out_g = 3 * (1 - odd_c), 3 * odd_c
    far_x, far_g = 3 * odd_c, 3 * (1 - odd_c)
    quarter = half // 2
    first_units = [(1, 0), (1, 1), (0, 0), (0, 1)]

    def exchange(units, sources, targets, relays):
        made = {}
        for n, unit in enumerate(units):
            sx, sg1, sg2 = sources(*unit)
            tx, tg1, tg2 = targets(*unit)
            made[unit] = (
                net.make(sx, tx, col=col_x),
                net.make(sg1, tg1, col=col_g, sends=has_g, gets=has_g),
                net.make(sg2, relays.at[n], col=col_r, sends=has_g, gets=has_r),
                net.make(relays.at[n], tg2, col=col_x, sends=has_r, gets=has_g),
            )
        return made

    def push(copies):
        copies[2].start()
        copies[0].start()
        copies[1].start()

    def hand_on(copies):
        copies[2].arrived()
        copies[3].start()

    def first_sources(which, part):
        start = half + rows_of(which)
        return (ext.at[part, edge_x, at(start, half), :],
                ext.at[part, edge_g, at(start, quarter), :],
                ext.at[part, edge_g, at(start + quarter, quarter), :])

    def first_targets(which, part):
        start = half + rows_of(which)
        return (ext.at[part, far_x, at(start, half), :],
                ext.at[part, far_g, at(start, quarter), :],
                ext.at[part, far_g, at(start + quarter, quarter), :])

    side = exchange(first_units, first_sources, first_targets, relay_in)
    def straight(unit):
        side[unit][0].start()
        side[unit][1].start()

    for unit in first_units:
        side[unit][2].start()
    for unit in first_units[:3]:
        straight(unit)

    def reorder(full):
        part = dot(jnp.concatenate(split3(full), axis=1), right[4])
        return dot(left[4], jnp.concatenate(split3(part), axis=0))

    def reorder_pats(p, carry):
        pats[p] = reorder(pats[p])
        return carry

    for copy in (pats_load, left_load, right_load, coeffs_load, probe_load):
        copy.wait()
    lax.fori_loop(0, count // 2, reorder_pats, 0)
    hand_on(side[first_units[0]])
    hand_on(side[first_units[1]])
    straight(first_units[3])
    lax.fori_loop(count // 2, count, reorder_pats, 0)
    hand_on(side[first_units[2]])
    hand_on(side[first_units[3]])
    for i in range(3):
        full = reorder(acc[i])
        for parity in (0, 1):
            coeffs[parity, i] = full[:, parity * LANES:(parity + 1) * LANES]

    corners = []

    def corner(unit, arrivals, b, has):
        which, part = unit
        for i in arrivals:
            side[unit][i].arrived()
        cond = both(has, side_has[which])
        mine = at(half + rows_of(which), half)
        there = at(side_row(which), half)
        corners.append(net.make(ext.at[part, b, mine, :], ext.at[part, b, there, :],
                                row=side_dev[which], sends=cond, gets=cond).start())

    for pair in (first_units[:2], first_units[2:]):
        for unit in pair:
            corner(unit, (0,), out_x, None)
        for unit in pair:
            corner(unit, (1, 3), out_g, has_g)
    for copy in ends + corners:
        copy.arrived()

    lane = lax.broadcasted_iota(jnp.int32, (1, LANES), 1)

    def place(p):
        oy, ox = offs[0, 0, 0, p], offs[0, 0, 1, p]
        block = lax.div(ox, LANES)
        return oy, block, ox - block * LANES

    def forward(source):
        def visit(p, carry):
            oy, block, shift = place(p)
            window = []
            keep = lane < LANES - shift
            for part in (0, 1):
                turned = [
                    pltpu.roll(source[part, block + j, pl.ds(oy, width), :], lax.rem(LANES - shift, LANES), axis=1)
                    for j in range(3)
                ]
                window.append([jnp.where(keep, turned[j], turned[j + 1]) for j in (0, 1)])
            sums, difs = [[], []], [[], []]
            for h in (0, 1):
                pr, pi = probe[0, :, h * LANES:(h + 1) * LANES], probe[1, :, h * LANES:(h + 1) * LANES]
                wr, wi = window[0][h], window[1][h]
                for part, x in ((0, pr * wr - pi * wi), (1, pr * wi + pi * wr)):
                    sums[part].append(x[:half] + x[half:])
                    difs[part].append(x[:half] - x[half:])
            bands = []
            for parity, group in ((0, sums), (1, difs)):
                stack = jnp.concatenate([jnp.concatenate(group[part], axis=1) for part in (0, 1)], axis=0)
                bands.append(from_left(left[parity], stack))
            re = jnp.concatenate([bands[0][:half], bands[1][:half]], axis=0)
            im = jnp.concatenate([bands[0][half:], bands[1][half:]], axis=0)
            plus = jnp.concatenate([re[:, :half] + re[:, half:], im[:, :half] + im[:, half:]], axis=1)
            minus = jnp.concatenate([re[:, :half] - re[:, half:], im[:, :half] - im[:, half:]], axis=1)
            for parity, full in ((0, plus), (1, minus)):
                highs[p, parity], lows[p, parity] = split(full)
            return carry

        lax.fori_loop(0, count, visit, 0, unroll=True)

    def finish_forward(parity, into):
        def visit(p, carry):
            high, low = highs[p, parity], lows[p, parity]
            into[p, parity] = dot(jnp.concatenate([high, low, high], axis=1), right[parity])
            return carry

        lax.fori_loop(0, count, visit, 0, unroll=True)

    def detect(turn, parity, response, rate):
        span = slice(parity * LANES, (parity + 1) * LANES)

        def chunk(i, carry):
            here = pl.ds(pl.multiple_of(i * CHUNK, CHUNK), CHUNK)
            lin, quad, cubic = (response[parity, j, here, :] for j in range(3))
            sums = [jnp.zeros((CHUNK, LANES), F32)] * 6
            for p in range(count):
                wr, wi = psi[p, parity, here, :LANES], psi[p, parity, here, LANES:]
                if rate is not None:
                    wr -= rate * phi[p, parity, here, :LANES]
                    wi -= rate * phi[p, parity, here, LANES:]
                inten = wr * wr + wi * wi
                error = inten * (lin + inten * (quad + inten * cubic)) - pats[p, here, span]
                weight = 2.0 * error * (lin + inten * (2.0 * quad + 3.0 * cubic * inten))
                squared = inten * inten
                cubed = squared * inten
                terms = (error * inten, error * squared, error * cubed,
                         squared, squared * squared, cubed * cubed)
                sums = [a + b for a, b in zip(sums, terms)]
                for j, part in ((0, weight * wr), (1, weight * wi)):
                    high, low = split(part)
                    highs[p, parity, here, j * LANES:(j + 1) * LANES] = high
                    lows[p, parity, here, j * LANES:(j + 1) * LANES] = low
            for j in range(6):
                stats[turn, parity, j, here, :] = sums[j]
            return carry

        lax.fori_loop(0, width // CHUNK, chunk, 0, unroll=2)

    def backward():
        def visit(p, carry):
            _, _, shift = place(p)
            bands = []
            for parity in (0, 1):
                high, low = highs[p, parity], lows[p, parity]
                bands.append(dot(jnp.concatenate([high, low, high], axis=1), right[2 + parity]))
            plus, minus = bands[0] + bands[1], bands[0] - bands[1]
            re = jnp.concatenate([plus[:, :half], minus[:, :half]], axis=1)
            im = jnp.concatenate([plus[:, half:], minus[:, half:]], axis=1)
            bands = []
            for parity in (0, 1):
                rows_in = slice(parity * half, (parity + 1) * half)
                bands.append(from_left(left[2 + parity], jnp.concatenate([re[rows_in], im[rows_in]], axis=0)))
            plus, minus = bands[0] + bands[1], bands[0] - bands[1]
            xr = jnp.concatenate([plus[:half], minus[:half]], axis=0)
            xi = jnp.concatenate([plus[half:], minus[half:]], axis=0)
            pr, pi = probe[0], probe[1]
            keep = lane >= shift
            for part, g in ((0, pr * xr + pi * xi), (1, pr * xi - pi * xr)):
                a = pltpu.roll(g[:, :LANES], shift, axis=1)
                b = pltpu.roll(g[:, LANES:], shift, axis=1)
                zero = jnp.zeros_like(a)
                pads[p, part, 1, pl.ds(width, width), :] = jnp.where(keep, a, zero)
                pads[p, part, 2, pl.ds(width, width), :] = jnp.where(keep, b, a)
                pads[p, part, 3, pl.ds(width, width), :] = jnp.where(keep, zero, b)
            return carry

        lax.fori_loop(0, count, visit, 0, unroll=True)

    def gather(turn, start, length):
        for part in (0, 1):
            for b in range(4):
                total = 0.0
                for p in range(count):
                    oy, block, _ = place(p)
                    total += pads[p, part, b + 1 - block, pl.ds(width - oy + start, length), :]
                grads[turn, part, b, pl.ds(start, length), :] = total

    rows1 = width // 2
    rows2, rows3 = shard.shape[3], z_sums.shape[4]
    cut = rows3 < rows2

    class Sums:
        def __init__(self, turn, parity, old):
            self.at, self.old = (turn, parity), old
            self.base2 = k * rows1 + c * rows2
            self.base3 = self.base2 + z * rows3 if cut else self.base2

        def pair(self):
            t = self.at
            self.first = net.make(stats.at[*t, :, at((1 - k) * rows1, rows1), :], half_sums.at[t], row=partner).start()

        def over_cols(self):
            t = self.at
            self.first.arrived()
            half_sums[t] += stats[*t, :, at(k * rows1, rows1), :]
            self.copies = []
            for d in range(1, cols):
                other = lax.rem(c + d, cols)
                self.copies.append(net.make(half_sums.at[*t, :, at(other * rows2, rows2), :],
                                            col_sums.at[*t, d - 1], col=other).start())

        def over_z(self):
            t = self.at
            for copy in self.copies:
                copy.arrived()
            shard[t] = half_sums[*t, :, at(c * rows2, rows2), :] + sum(col_sums[*t, d] for d in range(cols - 1))
            self.copies = []
            for d in range(1, depth):
                other = lax.rem(z + d, depth)
                source = shard.at[*t, :, at(other * rows3, rows3), :] if cut else shard.at[t]
                self.copies.append(net.make(source, z_sums.at[*t, d - 1], row=2 * other + k).start())

        def update(self):
            t = self.at
            for copy in self.copies:
                copy.arrived()
            own = shard[*t, :, at(z * rows3, rows3), :] if cut else shard[t]
            sums = own + sum(z_sums[*t, i] for i in range(depth - 1))
            new_coeffs[*t, :, at(self.base3, rows3), :] = (
                self.old[t[1], :, at(self.base3, rows3), :] - sums[:3] / (sums[3:] + RIDGE))
            self.copies = []
            if cut:
                ready = new_coeffs.at[*t, :, at(self.base3, rows3), :]
                for d in range(1, depth):
                    self.copies.append(net.make(ready, ready, row=2 * lax.rem(z + d, depth) + k).start())

        def spread(self):
            for copy in self.copies:
                copy.arrived()
            ready = new_coeffs.at[*self.at, :, at(self.base2, rows2), :]
            self.copies = [net.make(ready, ready, col=lax.rem(c + d, cols)).start() for d in range(1, cols)]

        def swap(self):
            for copy in self.copies:
                copy.arrived()
            ready = new_coeffs.at[*self.at, :, at(k * rows1, rows1), :]
            self.end = net.make(ready, ready, row=partner).start()

        def done(self):
            self.end.arrived()

    class Norm:
        def __init__(self, turn):
            self.turn = turn

        def pair(self, square):
            t = self.turn
            sq_mine[t] = square
            self.first = net.make(sq_mine.at[t], sq_pair.at[t], row=partner).start()

        def wide(self):
            t = self.turn
            self.first.arrived()
            sq_part[t] = sq_mine[t] + sq_pair[t]
            self.copies = []
            for i, place in enumerate(others):
                row, col = chip(*place)
                self.copies.append(net.make(sq_part.at[t], sq_all.at[t, i], row=row, col=col).start())

        def rate(self):
            t = self.turn
            for copy in self.copies:
                copy.arrived()
            square = sq_part[t] + sum(sq_all[t, i] for i in range(len(others)))
            total = 2.0 * tile * tile * rows * cols
            return STEP_RATE / jnp.sqrt(jnp.sum(square, keepdims=True) / total + EPSILON)

    def fold_rows(turn):
        made = {}
        for which in (1, 0):
            for part in (0, 1):
                made[(which, part)] = net.make(
                    grads.at[turn, part, :, at(edge_row(which), half), :], folds.at[turn, which, part],
                    row=side_dev[which], sends=side_has[which], gets=side_has[which],
                ).start()
        return made

    def add_fold(turn, made, which, part):
        made[(which, part)].arrived()

        def add():
            grads[turn, part, :, at(half + rows_of(which), half), :] += folds[turn, which, part]

        when(side_has[which], add)

    block_x, block_g = 2 * (1 - odd_c), 2 * odd_c

    forward(ext)
    sums0 = [Sums(0, parity, coeffs) for parity in (0, 1)]
    finish_forward(0, psi)
    detect(0, 0, coeffs, None)
    sums0[0].pair()
    finish_forward(1, psi)
    detect(0, 1, coeffs, None)
    sums0[1].pair()
    sums0[0].over_cols()
    backward()
    sums0[1].over_cols()
    gather(0, 0, half)
    gather(0, top, half)
    made = fold_rows(0)
    gather(0, half, tile)

    units = [(0, 0), (1, 0), (1, 1), (0, 1)]

    def mid_sources(which, part):
        here = at(half + rows_of(which), half)
        return (grads.at[0, part, pl.ds(block_x, 2), here, :],
                grads.at[0, part, block_g, here, :],
                grads.at[0, part, block_g + 1, here, :])

    def mid_targets(which, part):
        return got_x.at[which, part], got_g.at[which, part, 0], got_g.at[which, part, 1]

    mids = exchange(units, mid_sources, mid_targets, relay_g)
    sides = []

    def take(unit):
        which, part = unit
        here = at(half + rows_of(which), half)
        mids[unit][0].arrived()
        gext[part, pl.ds(block_x, 2), here, :] = grads[0, part, pl.ds(block_x, 2), here, :] + got_x[which, part]
        mids[unit][1].arrived()
        mids[unit][3].arrived()

        @pl.when(has_g)
        def _():
            gext[part, pl.ds(block_g, 2), here, :] = grads[0, part, pl.ds(block_g, 2), here, :] + got_g[which, part]

        @pl.when(jnp.logical_not(has_g))
        def _():
            gext[part, edge_g, here, :] = grads[0, part, edge_g, here, :]

        sides.append(net.make(
            gext.at[part, :, here, :], gext.at[part, :, at(side_row(which), half), :],
            row=side_dev[which], sends=side_has[which], gets=side_has[which],
        ).start())

    add_fold(0, made, *units[0])
    push(mids[units[0]])
    sums0[0].over_z()
    add_fold(0, made, *units[1])
    push(mids[units[1]])
    hand_on(mids[units[0]])
    for unit in units[2:]:
        add_fold(0, made, *unit)
        push(mids[unit])
    sums0[0].update()
    sums0[1].over_z()
    for unit in units[1:]:
        hand_on(mids[unit])
    take(units[0])
    sums0[0].spread()
    sums0[1].update()
    take(units[1])
    take(units[2])
    sums0[1].spread()
    take(units[3])

    def squares(blocks):
        total = 0.0
        for block in blocks:
            total += jnp.sum((block * block).reshape(-1, 8, LANES), axis=0)
        return total

    norm0 = Norm(0)
    mark = len(net.made)
    norm0.pair(squares([gext[part, b, inner, :] for part in (0, 1) for b in (1, 2)]))
    for copy in sides:
        copy.arrived()
    norm0.wide()

    sums0[0].swap()
    forward(gext)
    sums0[1].swap()
    finish_forward(0, phi)
    net.finish(mark)
    rate0 = norm0.rate()
    sums0[0].done()
    sums1 = [Sums(1, parity, new_coeffs.at[0]) for parity in (0, 1)]
    detect(1, 0, new_coeffs.at[0], rate0)
    sums1[0].pair()
    finish_forward(1, phi)
    sums0[1].done()
    detect(1, 1, new_coeffs.at[0], rate0)
    sums1[1].pair()
    sums1[0].over_cols()
    backward()
    sums1[1].over_cols()
    gather(1, 0, half)
    gather(1, top, half)
    made = fold_rows(1)
    gather(1, half, tile)

    units = [(0, 0), (0, 1), (1, 0), (1, 1)]

    def last_sources(which, part):
        start = half + rows_of(which)
        return (grads.at[1, part, out_x, at(start, half), :],
                grads.at[1, part, out_g, at(start, quarter), :],
                grads.at[1, part, out_g, at(start + quarter, quarter), :])

    def last_targets(which, part):
        return (last_x.at[which, part], last_g.at[which, part, pl.ds(0, quarter), :],
                last_g.at[which, part, pl.ds(quarter, quarter), :])

    lasts = exchange(units, last_sources, last_targets, relay_last)
    for part in (0, 1):
        for b in (0, 1):
            base[part, b] = ext[part, 1 + b, inner, :] - rate0 * gext[part, 1 + b, inner, :]
    def settle(unit):
        which, part = unit
        here = at(half + rows_of(which), half)
        there = at(rows_of(which), half)
        lasts[(which, part)][0].arrived()
        lasts[(which, part)][1].arrived()
        lasts[(which, part)][3].arrived()
        mine = grads[1, part, edge_x, here, :] + last_x[which, part]
        gtile[part, edge_x - 1, there, :] = mine
        square = squares([mine])

        @pl.when(has_g)
        def _():
            gtile[part, edge_g - 1, there, :] = grads[1, part, edge_g, here, :] + last_g[which, part]

        @pl.when(jnp.logical_not(has_g))
        def _():
            gtile[part, edge_g - 1, there, :] = grads[1, part, edge_g, here, :]

        return square + squares([gtile[part, edge_g - 1, there, :]])

    for unit in units[:2]:
        add_fold(1, made, *unit)
        push(lasts[unit])
    sums1[0].over_z()
    add_fold(1, made, *units[2])
    push(lasts[units[2]])
    hand_on(lasts[units[0]])
    hand_on(lasts[units[1]])
    sums1[0].update()
    add_fold(1, made, *units[3])
    push(lasts[units[3]])
    sums1[1].over_z()
    hand_on(lasts[units[2]])
    mark = len(net.made)
    sums1[0].spread()
    hand_on(lasts[units[3]])
    sums1[1].update()
    square = 0.0
    for unit in units:
        square += settle(unit)
    norm1 = Norm(1)
    norm1.pair(square)
    sums1[1].spread()
    norm1.wide()
    sums1[0].swap()
    net.finish(mark)
    rate1 = norm1.rate()
    for part in (0, 1):
        for b in (0, 1):
            field_out[part, :, b * LANES:(b + 1) * LANES] = base[part, b] - rate1 * gtile[part, b]
    sums1[0].done()

    def natural(i, parity):
        begin = parity * LANES
        spread = jnp.concatenate([right[5, j * width + begin:j * width + begin + LANES, :] for j in range(3)], axis=0)
        return dot(jnp.concatenate(split3(new_coeffs[1, parity, i]), axis=1), spread)

    for i in range(3):
        acc[i] = natural(i, 0)
    sums1[1].swap()
    sums1[1].done()
    for i in range(3):
        full = acc[i] + natural(i, 1)
        for b in (0, 1):
            span = slice(b * LANES, (b + 1) * LANES)
            for parity in (0, 1):
                woven[i, b, pl.ds(parity, half, stride=2), :] = full[parity * half:(parity + 1) * half, span]
            coeffs_out[i, :, span] = woven[i, b]
    net.finish()


def local(object_field, probe, coeffs, patterns, offsets):
    rows, cols = lax.axis_size("row"), lax.axis_size("col")
    depth = rows // 2
    count, width = patterns.shape[2], probe.shape[1]
    half = width // 2
    tile = object_field.shape[1]
    size = tile + width
    rows1 = width // 2
    rows2 = rows1 // cols
    rows3 = rows2 // depth if rows2 % (8 * depth) == 0 else rows2
    left, right = dft_halves(width)
    vmem = pl.BlockSpec(memory_space=pltpu.VMEM)
    hbm = pl.BlockSpec(memory_space=pltpu.HBM)
    semaphores = copies_needed(rows, cols)
    extended = (2, size // LANES, size, LANES)
    freq = (count, 2, width, width)
    refined = pl.pallas_call(
        refine_kernel,
        out_shape=(
            jax.ShapeDtypeStruct((2, tile, tile), F32),
            jax.ShapeDtypeStruct(coeffs.shape, F32),
        ),
        in_specs=[hbm] * 4 + [pl.BlockSpec(memory_space=pltpu.SMEM)] + [hbm] * 2,
        out_specs=(vmem, vmem),
        scratch_shapes=[
            pltpu.VMEM(extended, F32),
            pltpu.VMEM((2,) + extended, F32),
            pltpu.VMEM(extended, F32),
            pltpu.VMEM((count, 2, 5, 3 * width, LANES), F32),
            pltpu.VMEM(freq, F32),
            pltpu.VMEM(freq, F32),
            pltpu.VMEM(freq, BF16),
            pltpu.VMEM(freq, BF16),
            pltpu.VMEM((2, width, width), F32),
            pltpu.VMEM((2, 3, width, LANES), F32),
            pltpu.VMEM((count, width, width), F32),
            pltpu.VMEM(left.shape, BF16),
            pltpu.VMEM(right.shape, BF16),
            pltpu.VMEM((2, 2, 6, width, LANES), F32),
            pltpu.VMEM((2, 2, 6, rows1, LANES), F32),
            pltpu.VMEM((2, 2, cols - 1, 6, rows2, LANES), F32),
            pltpu.VMEM((2, 2, 6, rows2, LANES), F32),
            pltpu.VMEM((2, 2, depth - 1, 6, rows3, LANES), F32),
            pltpu.VMEM((2, 2, 3, width, LANES), F32),
            pltpu.VMEM((2, 2, 2, size // LANES, half, LANES), F32),
            pltpu.VMEM((2, 2, 2, half, LANES), F32),
            pltpu.VMEM((2, 2, 2, half, LANES), F32),
            pltpu.VMEM((4, half // 2, LANES), F32),
            pltpu.VMEM((4, half, LANES), F32),
            pltpu.VMEM((2, 2, half, LANES), F32),
            pltpu.VMEM((2, 2, half, LANES), F32),
            pltpu.VMEM((4, half // 2, LANES), F32),
            pltpu.VMEM((2, 2, tile, LANES), F32),
            pltpu.VMEM((2, 2, tile, LANES), F32),
            pltpu.VMEM((2, 8, LANES), F32),
            pltpu.VMEM((2, 8, LANES), F32),
            pltpu.VMEM((2, 8, LANES), F32),
            pltpu.VMEM((2, depth * cols - 1, 8, LANES), F32),
            pltpu.VMEM((3, width // LANES, width, LANES), F32),
            pltpu.VMEM((3, width, width), F32),
            pltpu.SemaphoreType.DMA((8,)),
            pltpu.SemaphoreType.DMA((semaphores,)),
            pltpu.SemaphoreType.DMA((semaphores,)),
        ],
        compiler_params=pltpu.CompilerParams(
            collective_id=0, has_side_effects=True, vmem_limit_bytes=60 * 1024 * 1024
        ),
        name="refine",
    )(object_field, probe, coeffs, patterns, jnp.swapaxes(offsets, 2, 3), left, right)
    return close(*refined)


def close_kernel(field, coeffs, field_out, coeffs_out, held, sems):
    planes = [(field.at[i], field_out.at[i]) for i in range(field.shape[0])]
    planes += [(coeffs.at[i], coeffs_out.at[i]) for i in range(coeffs.shape[0])]
    copies = [
        (pltpu.make_async_copy(source, held.at[n], sems.at[0, n]), pltpu.make_async_copy(held.at[n], target, sems.at[1, n]))
        for n, (source, target) in enumerate(planes)
    ]
    for come, _ in copies:
        come.start()
    for come, go in copies:
        come.wait()
        go.start()
    for _, go in copies:
        go.wait()


def close(field, coeffs):
    hbm = pl.BlockSpec(memory_space=pl.ANY)
    count = field.shape[0] + coeffs.shape[0]
    return pl.pallas_call(
        close_kernel,
        out_shape=tuple(jax.ShapeDtypeStruct(a.shape, a.dtype) for a in (field, coeffs)),
        in_specs=[hbm] * 2,
        out_specs=(hbm, hbm),
        scratch_shapes=[pltpu.VMEM((count,) + field.shape[1:], F32), pltpu.SemaphoreType.DMA((2, count))],
        compiler_params=pltpu.CompilerParams(vmem_limit_bytes=60 * 1024 * 1024),
        name="close",
    )(field, coeffs)


def solution(mesh):
    placed = (
        P(None, "row", "col"),
        P(),
        P(),
        P("row", "col", None, None, None),
        P("row", "col", None, None),
    )
    return jax.shard_map(
        local, mesh=mesh, in_specs=placed, out_specs=(P(None, "row", "col"), P()), check_vma=False
    )
```

```python
import functools

import jax
import jax.numpy as jnp
import ml_dtypes
import numpy as np
from jax import lax
from jax.experimental import pallas as pl
from jax.experimental.pallas import tpu as pltpu
from jax.sharding import PartitionSpec as P

STEP_RATE = 0.2
RIDGE = 1.0
EPSILON = 1e-06
LANES = 128
CHUNK = 16
F32 = jnp.float32
BF16 = jnp.bfloat16


def dft_halves(order):
    half = order // 2
    index = np.arange(order)
    angle = -2.0 * np.pi / order * (index[:, None] * index[None, :] % order)
    real, imag = np.cos(angle) / np.sqrt(order), np.sin(angle) / np.sqrt(order)
    lefts, rights = [], []
    for parity in (0, 1):
        re, im = real[parity::2, :half], imag[parity::2, :half]
        full = np.block([[re, -im], [im, re]]).astype(np.float32)
        for into, forward in ((lefts, full), (rights, full.T)):
            high = forward.astype(ml_dtypes.bfloat16)
            low = (forward - high.astype(np.float32)).astype(ml_dtypes.bfloat16)
            into.append((high, low))
    wide = lambda pair: np.concatenate([pair[0], pair[0], pair[1]], axis=1)
    tall = lambda pair: np.concatenate([pair[0], pair[0], pair[1]], axis=0)
    on_left = [wide(m) for m in lefts] + [wide(m) for m in rights]
    on_right = [tall(m) for m in rights] + [tall(m) for m in lefts]
    order_of = np.concatenate([index[0::2], index[1::2]])
    perm = (order_of[:, None] == index[None, :]).astype(ml_dtypes.bfloat16)
    on_left.append(np.concatenate([perm] * 3, axis=1))
    on_right.append(np.concatenate([perm.T] * 3, axis=0))
    on_right.append(np.concatenate([perm] * 3, axis=0))
    return jnp.asarray(np.stack(on_left)), jnp.asarray(np.stack(on_right))


def dot(left, right):
    return jnp.dot(left, right, preferred_element_type=F32)


def split(full):
    high = full.astype(BF16)
    return high, (full - high.astype(F32)).astype(BF16)


def split3(full):
    high = full.astype(BF16)
    rest = full - high.astype(F32)
    mid = rest.astype(BF16)
    return high, mid, (rest - mid.astype(F32)).astype(BF16)


def from_left(matrix, full):
    high, low = split(full)
    return dot(matrix, jnp.concatenate([high, low, high], axis=0))


class Copies:
    def __init__(self, send, recv):
        self.send, self.recv, self.used, self.made, self.ended = send, recv, 0, [], 0

    def make(self, source, target, row=None, col=None, sends=None, gets=None):
        slot = self.used
        self.used += 1
        where = (lax.axis_index("row") if row is None else row, lax.axis_index("col") if col is None else col)
        copy = pltpu.make_async_remote_copy(
            src_ref=source, dst_ref=target, send_sem=self.send.at[slot], recv_sem=self.recv.at[slot],
            device_id=where, device_id_type=pl.DeviceIdType.MESH,
        )
        made = Copy(copy, sends, gets)
        self.made.append(made)
        return made

    def finish(self, mark=None):
        mark = len(self.made) if mark is None else mark
        for made in self.made[self.ended:mark]:
            made.sent()
        self.ended = mark


def when(condition, act):
    if condition is None:
        act()
    else:
        pl.when(condition)(act)


class Copy:
    def __init__(self, copy, sends, gets):
        self.copy, self.sends, self.gets = copy, sends, gets

    def start(self):
        when(self.sends, self.copy.start)
        return self

    def arrived(self):
        when(self.gets, self.copy.wait_recv)

    def sent(self):
        when(self.sends, self.copy.wait_send)


def both(a, b):
    return b if a is None else a if b is None else a & b


def copies_needed(rows, cols):
    return 160 + 4 * (rows + cols) + rows * cols


def refine_kernel(field_hbm, probe_hbm, coeffs_hbm, pats_hbm, offs, left_hbm, right_hbm,
                  field_out, coeffs_out,
                  ext, grads, gext, pads, psi, phi, highs, lows, probe, coeffs, pats, left, right,
                  stats, half_sums, col_sums, shard, z_sums, new_coeffs,
                  folds, got_x, got_g, relay_in, relay_g, last_x, last_g, relay_last, base, gtile,
                  sq_mine, sq_pair, sq_part, sq_all, woven, acc,
                  local_sem, send_sem, recv_sem):
    rows, cols = lax.axis_size("row"), lax.axis_size("col")
    r, c = lax.axis_index("row"), lax.axis_index("col")
    depth = rows // 2
    k, z = lax.rem(r, 2), lax.div(r, 2)
    count = pats.shape[0]
    width = probe.shape[1]
    half = width // 2
    size = ext.shape[2]
    tile = size - width
    top = half + tile
    net = Copies(send_sem, recv_sem)

    partner = r + 1 - 2 * k
    beyond = r - 1 + 2 * k
    has_z = (beyond >= 0) & (beyond < rows)
    beyond = lax.rem(beyond + rows, rows)
    odd_c = lax.rem(c, 2)
    step_g = 2 * odd_c - 1
    has_g = (c + step_g >= 0) & (c + step_g < cols)
    has_r = (c - 2 * step_g >= 0) & (c - 2 * step_g < cols)
    col_x = c - step_g
    col_g = lax.rem(c + step_g + cols, cols)
    col_r = lax.rem(c + 2 * step_g + 2 * cols, cols)

    def chip(dz, dc):
        return 2 * lax.rem(z + dz, depth) + k, lax.rem(c + dc, cols)

    others = [(dz, dc) for dz in range(depth) for dc in range(cols) if dz or dc]

    barrier = pltpu.get_barrier_semaphore()

    def greet(row, col):
        pl.semaphore_signal(barrier, inc=1, device_id=(row, col), device_id_type=pl.DeviceIdType.MESH)

    near = [(0, dc) for dc in range(1, cols)] + [(dz, 0) for dz in range(1, depth)]
    when(has_z, lambda: greet(beyond, c))
    greet(partner, c)
    for dz, dc in near:
        greet(*chip(dz, dc))
    greeted = len(near) + 1 + has_z.astype(jnp.int32)

    inner = pl.ds(half, tile)
    loads = []

    def load(source, target):
        copy = pltpu.make_async_copy(source, target, local_sem.at[len(loads)])
        copy.start()
        loads.append(copy)
        return copy

    field_loads = [
        load(field_hbm.at[:, :, pl.ds(b * LANES, LANES)], ext.at[:, 1 + b, inner, :]) for b in (0, 1)
    ]
    pats_load = load(pats_hbm.at[0, 0], pats)
    coeffs_load = load(coeffs_hbm, acc)
    left_load = load(left_hbm, left)
    right_load = load(right_hbm, right)
    probe_load = load(probe_hbm, probe)

    for edge, b in ((c == 0, 0), (c == cols - 1, 3)):
        @pl.when(edge)
        def _():
            ext[:, b] = jnp.zeros((2, size, LANES), F32)
            gext[:, b] = jnp.zeros((2, size, LANES), F32)
    for edge, start in ((r == 0, 0), (r == rows - 1, top)):
        @pl.when(edge)
        def _():
            ext[:, :, pl.ds(start, half), :] = jnp.zeros((2, 4, half, LANES), F32)
            gext[:, :, pl.ds(start, half), :] = jnp.zeros((2, 4, half, LANES), F32)

    def clear(p, carry):
        for part in (0, 1):
            for b in (0, 4):
                pads[p, part, b] = jnp.zeros((3 * width, LANES), F32)
            for b in (1, 2, 3):
                for start in (0, 2 * width):
                    pads[p, part, b, pl.ds(start, width), :] = jnp.zeros((width, LANES), F32)
        return carry

    for copy in field_loads:
        copy.wait()
    pl.semaphore_wait(barrier, greeted)

    def rows_of(which):
        return half * (1 - k) if which == 0 else half * k

    def side_row(which):
        return top * k if which == 0 else top * (1 - k)

    def edge_row(which):
        return top * (1 - k) if which == 0 else top * k

    def at(start, length):
        return pl.ds(pl.multiple_of(start, 8), length)

    side_dev = (partner, beyond)
    side_has = (None, has_z)

    ends = []
    for which in (1, 0):
        mine = at(half + rows_of(which), half)
        there = at(side_row(which), half)
        ends.append(net.make(ext.at[:, pl.ds(1, 2), mine, :], ext.at[:, pl.ds(1, 2), there, :],
                             row=side_dev[which], sends=side_has[which], gets=side_has[which]).start())

    edge_x, edge_g = 2 - odd_c, 1 + odd_c
    out_x, out_g = 3 * (1 - odd_c), 3 * odd_c
    far_x, far_g = 3 * odd_c, 3 * (1 - odd_c)
    quarter = half // 2
    first_units = [(1, 0), (1, 1), (0, 0), (0, 1)]

    def exchange(units, sources, targets, relays):
        made = {}
        for n, unit in enumerate(units):
            sx, sg1, sg2 = sources(*unit)
            tx, tg1, tg2 = targets(*unit)
            made[unit] = (
                net.make(sx, tx, col=col_x),
                net.make(sg1, tg1, col=col_g, sends=has_g, gets=has_g),
                net.make(sg2, relays.at[n], col=col_r, sends=has_g, gets=has_r),
                net.make(relays.at[n], tg2, col=col_x, sends=has_r, gets=has_g),
            )
        return made

    def push(copies):
        copies[2].start()
        copies[0].start()
        copies[1].start()

    def hand_on(copies):
        copies[2].arrived()
        copies[3].start()

    def first_sources(which, part):
        start = half + rows_of(which)
        return (ext.at[part, edge_x, at(start, half), :],
                ext.at[part, edge_g, at(start, quarter), :],
                ext.at[part, edge_g, at(start + quarter, quarter), :])

    def first_targets(which, part):
        start = half + rows_of(which)
        return (ext.at[part, far_x, at(start, half), :],
                ext.at[part, far_g, at(start, quarter), :],
                ext.at[part, far_g, at(start + quarter, quarter), :])

    side = exchange(first_units, first_sources, first_targets, relay_in)
    def straight(unit):
        side[unit][0].start()
        side[unit][1].start()

    for unit in first_units:
        side[unit][2].start()
    for unit in first_units[:3]:
        straight(unit)
    lax.fori_loop(0, count, clear, 0)

    def reorder(full):
        part = dot(jnp.concatenate(split3(full), axis=1), right[4])
        return dot(left[4], jnp.concatenate(split3(part), axis=0))

    def reorder_pats(p, carry):
        pats[p] = reorder(pats[p])
        return carry

    for copy in (pats_load, left_load, right_load, coeffs_load, probe_load):
        copy.wait()
    lax.fori_loop(0, count // 2, reorder_pats, 0)
    hand_on(side[first_units[0]])
    hand_on(side[first_units[1]])
    straight(first_units[3])
    lax.fori_loop(count // 2, count, reorder_pats, 0)
    hand_on(side[first_units[2]])
    hand_on(side[first_units[3]])
    for i in range(3):
        full = reorder(acc[i])
        for parity in (0, 1):
            coeffs[parity, i] = full[:, parity * LANES:(parity + 1) * LANES]

    corners = []

    def corner(unit, arrivals, b, has):
        which, part = unit
        for i in arrivals:
            side[unit][i].arrived()
        cond = both(has, side_has[which])
        mine = at(half + rows_of(which), half)
        there = at(side_row(which), half)
        corners.append(net.make(ext.at[part, b, mine, :], ext.at[part, b, there, :],
                                row=side_dev[which], sends=cond, gets=cond).start())

    for pair in (first_units[:2], first_units[2:]):
        for unit in pair:
            corner(unit, (0,), out_x, None)
        for unit in pair:
            corner(unit, (1, 3), out_g, has_g)
    for copy in ends + corners:
        copy.arrived()

    lane = lax.broadcasted_iota(jnp.int32, (1, LANES), 1)

    def place(p):
        oy, ox = offs[0, 0, 0, p], offs[0, 0, 1, p]
        block = lax.div(ox, LANES)
        return oy, block, ox - block * LANES

    def forward(source):
        def visit(p, carry):
            oy, block, shift = place(p)
            window = []
            keep = lane < LANES - shift
            for part in (0, 1):
                turned = [
                    pltpu.roll(source[part, block + j, pl.ds(oy, width), :], lax.rem(LANES - shift, LANES), axis=1)
                    for j in range(3)
                ]
                window.append([jnp.where(keep, turned[j], turned[j + 1]) for j in (0, 1)])
            sums, difs = [[], []], [[], []]
            for h in (0, 1):
                pr, pi = probe[0, :, h * LANES:(h + 1) * LANES], probe[1, :, h * LANES:(h + 1) * LANES]
                wr, wi = window[0][h], window[1][h]
                for part, x in ((0, pr * wr - pi * wi), (1, pr * wi + pi * wr)):
                    sums[part].append(x[:half] + x[half:])
                    difs[part].append(x[:half] - x[half:])
            bands = []
            for parity, group in ((0, sums), (1, difs)):
                stack = jnp.concatenate([jnp.concatenate(group[part], axis=1) for part in (0, 1)], axis=0)
                bands.append(from_left(left[parity], stack))
            re = jnp.concatenate([bands[0][:half], bands[1][:half]], axis=0)
            im = jnp.concatenate([bands[0][half:], bands[1][half:]], axis=0)
            plus = jnp.concatenate([re[:, :half] + re[:, half:], im[:, :half] + im[:, half:]], axis=1)
            minus = jnp.concatenate([re[:, :half] - re[:, half:], im[:, :half] - im[:, half:]], axis=1)
            for parity, full in ((0, plus), (1, minus)):
                highs[p, parity], lows[p, parity] = split(full)
            return carry

        lax.fori_loop(0, count, visit, 0, unroll=True)

    def finish_forward(parity, into):
        def visit(p, carry):
            high, low = highs[p, parity], lows[p, parity]
            into[p, parity] = dot(jnp.concatenate([high, low, high], axis=1), right[parity])
            return carry

        lax.fori_loop(0, count, visit, 0, unroll=True)

    def detect(turn, parity, response, rate):
        span = slice(parity * LANES, (parity + 1) * LANES)

        def chunk(i, carry):
            here = pl.ds(pl.multiple_of(i * CHUNK, CHUNK), CHUNK)
            lin, quad, cubic = (response[parity, j, here, :] for j in range(3))
            sums = [jnp.zeros((CHUNK, LANES), F32)] * 6
            for p in range(count):
                wr, wi = psi[p, parity, here, :LANES], psi[p, parity, here, LANES:]
                if rate is not None:
                    wr -= rate * phi[p, parity, here, :LANES]
                    wi -= rate * phi[p, parity, here, LANES:]
                inten = wr * wr + wi * wi
                error = inten * (lin + inten * (quad + inten * cubic)) - pats[p, here, span]
                weight = 2.0 * error * (lin + inten * (2.0 * quad + 3.0 * cubic * inten))
                squared = inten * inten
                cubed = squared * inten
                terms = (error * inten, error * squared, error * cubed,
                         squared, squared * squared, cubed * cubed)
                sums = [a + b for a, b in zip(sums, terms)]
                for j, part in ((0, weight * wr), (1, weight * wi)):
                    high, low = split(part)
                    highs[p, parity, here, j * LANES:(j + 1) * LANES] = high
                    lows[p, parity, here, j * LANES:(j + 1) * LANES] = low
            for j in range(6):
                stats[turn, parity, j, here, :] = sums[j]
            return carry

        lax.fori_loop(0, width // CHUNK, chunk, 0, unroll=2)

    def backward():
        def visit(p, carry):
            _, _, shift = place(p)
            bands = []
            for parity in (0, 1):
                high, low = highs[p, parity], lows[p, parity]
                bands.append(dot(jnp.concatenate([high, low, high], axis=1), right[2 + parity]))
            plus, minus = bands[0] + bands[1], bands[0] - bands[1]
            re = jnp.concatenate([plus[:, :half], minus[:, :half]], axis=1)
            im = jnp.concatenate([plus[:, half:], minus[:, half:]], axis=1)
            bands = []
            for parity in (0, 1):
                rows_in = slice(parity * half, (parity + 1) * half)
                bands.append(from_left(left[2 + parity], jnp.concatenate([re[rows_in], im[rows_in]], axis=0)))
            plus, minus = bands[0] + bands[1], bands[0] - bands[1]
            xr = jnp.concatenate([plus[:half], minus[:half]], axis=0)
            xi = jnp.concatenate([plus[half:], minus[half:]], axis=0)
            pr, pi = probe[0], probe[1]
            keep = lane >= shift
            for part, g in ((0, pr * xr + pi * xi), (1, pr * xi - pi * xr)):
                a = pltpu.roll(g[:, :LANES], shift, axis=1)
                b = pltpu.roll(g[:, LANES:], shift, axis=1)
                zero = jnp.zeros_like(a)
                pads[p, part, 1, pl.ds(width, width), :] = jnp.where(keep, a, zero)
                pads[p, part, 2, pl.ds(width, width), :] = jnp.where(keep, b, a)
                pads[p, part, 3, pl.ds(width, width), :] = jnp.where(keep, zero, b)
            return carry

        lax.fori_loop(0, count, visit, 0, unroll=True)

    def gather(turn, start, length):
        for part in (0, 1):
            for b in range(4):
                total = 0.0
                for p in range(count):
                    oy, block, _ = place(p)
                    total += pads[p, part, b + 1 - block, pl.ds(width - oy + start, length), :]
                grads[turn, part, b, pl.ds(start, length), :] = total

    rows1 = width // 2
    rows2, rows3 = shard.shape[3], z_sums.shape[4]
    cut = rows3 < rows2

    class Sums:
        def __init__(self, turn, parity, old):
            self.at, self.old = (turn, parity), old
            self.base2 = k * rows1 + c * rows2
            self.base3 = self.base2 + z * rows3 if cut else self.base2

        def pair(self):
            t = self.at
            self.first = net.make(stats.at[*t, :, at((1 - k) * rows1, rows1), :], half_sums.at[t], row=partner).start()

        def over_cols(self):
            t = self.at
            self.first.arrived()
            half_sums[t] += stats[*t, :, at(k * rows1, rows1), :]
            self.copies = []
            for d in range(1, cols):
                other = lax.rem(c + d, cols)
                self.copies.append(net.make(half_sums.at[*t, :, at(other * rows2, rows2), :],
                                            col_sums.at[*t, d - 1], col=other).start())

        def over_z(self):
            t = self.at
            for copy in self.copies:
                copy.arrived()
            shard[t] = half_sums[*t, :, at(c * rows2, rows2), :] + sum(col_sums[*t, d] for d in range(cols - 1))
            self.copies = []
            for d in range(1, depth):
                other = lax.rem(z + d, depth)
                source = shard.at[*t, :, at(other * rows3, rows3), :] if cut else shard.at[t]
                self.copies.append(net.make(source, z_sums.at[*t, d - 1], row=2 * other + k).start())

        def update(self):
            t = self.at
            for copy in self.copies:
                copy.arrived()
            own = shard[*t, :, at(z * rows3, rows3), :] if cut else shard[t]
            sums = own + sum(z_sums[*t, i] for i in range(depth - 1))
            new_coeffs[*t, :, at(self.base3, rows3), :] = (
                self.old[t[1], :, at(self.base3, rows3), :] - sums[:3] / (sums[3:] + RIDGE))
            self.copies = []
            if cut:
                ready = new_coeffs.at[*t, :, at(self.base3, rows3), :]
                for d in range(1, depth):
                    self.copies.append(net.make(ready, ready, row=2 * lax.rem(z + d, depth) + k).start())

        def spread(self):
            for copy in self.copies:
                copy.arrived()
            ready = new_coeffs.at[*self.at, :, at(self.base2, rows2), :]
            self.copies = [net.make(ready, ready, col=lax.rem(c + d, cols)).start() for d in range(1, cols)]

        def swap(self):
            for copy in self.copies:
                copy.arrived()
            ready = new_coeffs.at[*self.at, :, at(k * rows1, rows1), :]
            self.end = net.make(ready, ready, row=partner).start()

        def done(self):
            self.end.arrived()

    class Norm:
        def __init__(self, turn):
            self.turn = turn

        def pair(self, square):
            t = self.turn
            sq_mine[t] = square
            self.first = net.make(sq_mine.at[t], sq_pair.at[t], row=partner).start()

        def wide(self):
            t = self.turn
            self.first.arrived()
            sq_part[t] = sq_mine[t] + sq_pair[t]
            self.copies = []
            for i, place in enumerate(others):
                row, col = chip(*place)
                self.copies.append(net.make(sq_part.at[t], sq_all.at[t, i], row=row, col=col).start())

        def rate(self):
            t = self.turn
            for copy in self.copies:
                copy.arrived()
            square = sq_part[t] + sum(sq_all[t, i] for i in range(len(others)))
            total = 2.0 * tile * tile * rows * cols
            return STEP_RATE / jnp.sqrt(jnp.sum(square, keepdims=True) / total + EPSILON)

    def fold_rows(turn):
        made = {}
        for which in (1, 0):
            gather(turn, pl.multiple_of(edge_row(which), 8), half)
            for part in (0, 1):
                made[(which, part)] = net.make(
                    grads.at[turn, part, :, at(edge_row(which), half), :], folds.at[turn, which, part],
                    row=side_dev[which], sends=side_has[which], gets=side_has[which],
                ).start()
        return made

    def add_fold(turn, made, which, part):
        made[(which, part)].arrived()

        def add():
            grads[turn, part, :, at(half + rows_of(which), half), :] += folds[turn, which, part]

        when(side_has[which], add)

    block_x, block_g = 2 * (1 - odd_c), 2 * odd_c

    forward(ext)
    sums0 = [Sums(0, parity, coeffs) for parity in (0, 1)]
    finish_forward(0, psi)
    detect(0, 0, coeffs, None)
    sums0[0].pair()
    finish_forward(1, psi)
    detect(0, 1, coeffs, None)
    sums0[1].pair()
    sums0[0].over_cols()
    backward()
    sums0[1].over_cols()
    made = fold_rows(0)
    gather(0, half, tile)

    units = [(0, 0), (1, 0), (1, 1), (0, 1)]

    def mid_sources(which, part):
        here = at(half + rows_of(which), half)
        return (grads.at[0, part, pl.ds(block_x, 2), here, :],
                grads.at[0, part, block_g, here, :],
                grads.at[0, part, block_g + 1, here, :])

    def mid_targets(which, part):
        return got_x.at[which, part], got_g.at[which, part, 0], got_g.at[which, part, 1]

    mids = exchange(units, mid_sources, mid_targets, relay_g)
    sides = []

    def take(unit):
        which, part = unit
        here = at(half + rows_of(which), half)
        mids[unit][0].arrived()
        gext[part, pl.ds(block_x, 2), here, :] = grads[0, part, pl.ds(block_x, 2), here, :] + got_x[which, part]
        mids[unit][1].arrived()
        mids[unit][3].arrived()

        @pl.when(has_g)
        def _():
            gext[part, pl.ds(block_g, 2), here, :] = grads[0, part, pl.ds(block_g, 2), here, :] + got_g[which, part]

        @pl.when(jnp.logical_not(has_g))
        def _():
            gext[part, edge_g, here, :] = grads[0, part, edge_g, here, :]

        sides.append(net.make(
            gext.at[part, :, here, :], gext.at[part, :, at(side_row(which), half), :],
            row=side_dev[which], sends=side_has[which], gets=side_has[which],
        ).start())

    add_fold(0, made, *units[0])
    push(mids[units[0]])
    sums0[0].over_z()
    add_fold(0, made, *units[1])
    push(mids[units[1]])
    hand_on(mids[units[0]])
    for unit in units[2:]:
        add_fold(0, made, *unit)
        push(mids[unit])
    sums0[0].update()
    sums0[1].over_z()
    for unit in units[1:]:
        hand_on(mids[unit])
    take(units[0])
    sums0[0].spread()
    sums0[1].update()
    take(units[1])
    take(units[2])
    sums0[1].spread()
    take(units[3])

    def squares(blocks):
        total = 0.0
        for block in blocks:
            total += jnp.sum((block * block).reshape(-1, 8, LANES), axis=0)
        return total

    norm0 = Norm(0)
    mark = len(net.made)
    norm0.pair(squares([gext[part, b, inner, :] for part in (0, 1) for b in (1, 2)]))
    for copy in sides:
        copy.arrived()
    norm0.wide()

    sums0[0].swap()
    forward(gext)
    sums0[1].swap()
    finish_forward(0, phi)
    net.finish(mark)
    rate0 = norm0.rate()
    sums0[0].done()
    sums1 = [Sums(1, parity, new_coeffs.at[0]) for parity in (0, 1)]
    detect(1, 0, new_coeffs.at[0], rate0)
    sums1[0].pair()
    finish_forward(1, phi)
    sums0[1].done()
    detect(1, 1, new_coeffs.at[0], rate0)
    sums1[1].pair()
    sums1[0].over_cols()
    backward()
    sums1[1].over_cols()
    made = fold_rows(1)
    gather(1, half, tile)

    units = [(0, 0), (0, 1), (1, 0), (1, 1)]

    def last_sources(which, part):
        start = half + rows_of(which)
        return (grads.at[1, part, out_x, at(start, half), :],
                grads.at[1, part, out_g, at(start, quarter), :],
                grads.at[1, part, out_g, at(start + quarter, quarter), :])

    def last_targets(which, part):
        return (last_x.at[which, part], last_g.at[which, part, pl.ds(0, quarter), :],
                last_g.at[which, part, pl.ds(quarter, quarter), :])

    lasts = exchange(units, last_sources, last_targets, relay_last)
    for part in (0, 1):
        for b in (0, 1):
            base[part, b] = ext[part, 1 + b, inner, :] - rate0 * gext[part, 1 + b, inner, :]
    def settle(unit):
        which, part = unit
        here = at(half + rows_of(which), half)
        there = at(rows_of(which), half)
        lasts[(which, part)][0].arrived()
        lasts[(which, part)][1].arrived()
        lasts[(which, part)][3].arrived()
        mine = grads[1, part, edge_x, here, :] + last_x[which, part]
        gtile[part, edge_x - 1, there, :] = mine
        square = squares([mine])

        @pl.when(has_g)
        def _():
            gtile[part, edge_g - 1, there, :] = grads[1, part, edge_g, here, :] + last_g[which, part]

        @pl.when(jnp.logical_not(has_g))
        def _():
            gtile[part, edge_g - 1, there, :] = grads[1, part, edge_g, here, :]

        return square + squares([gtile[part, edge_g - 1, there, :]])

    for unit in units[:2]:
        add_fold(1, made, *unit)
        push(lasts[unit])
    sums1[0].over_z()
    add_fold(1, made, *units[2])
    push(lasts[units[2]])
    hand_on(lasts[units[0]])
    hand_on(lasts[units[1]])
    sums1[0].update()
    add_fold(1, made, *units[3])
    push(lasts[units[3]])
    sums1[1].over_z()
    hand_on(lasts[units[2]])
    mark = len(net.made)
    sums1[0].spread()
    hand_on(lasts[units[3]])
    sums1[1].update()
    square = 0.0
    for unit in units:
        square += settle(unit)
    norm1 = Norm(1)
    norm1.pair(square)
    sums1[1].spread()
    norm1.wide()
    sums1[0].swap()
    net.finish(mark)
    rate1 = norm1.rate()
    for part in (0, 1):
        for b in (0, 1):
            field_out[part, :, b * LANES:(b + 1) * LANES] = base[part, b] - rate1 * gtile[part, b]
    sums1[0].done()

    def natural(i, parity):
        begin = parity * LANES
        spread = jnp.concatenate([right[5, j * width + begin:j * width + begin + LANES, :] for j in range(3)], axis=0)
        return dot(jnp.concatenate(split3(new_coeffs[1, parity, i]), axis=1), spread)

    for i in range(3):
        acc[i] = natural(i, 0)
    sums1[1].swap()
    sums1[1].done()
    for i in range(3):
        full = acc[i] + natural(i, 1)
        for b in (0, 1):
            span = slice(b * LANES, (b + 1) * LANES)
            for parity in (0, 1):
                woven[i, b, pl.ds(parity, half, stride=2), :] = full[parity * half:(parity + 1) * half, span]
            coeffs_out[i, :, span] = woven[i, b]
    net.finish()


def local(object_field, probe, coeffs, patterns, offsets):
    rows, cols = lax.axis_size("row"), lax.axis_size("col")
    depth = rows // 2
    count, width = patterns.shape[2], probe.shape[1]
    half = width // 2
    tile = object_field.shape[1]
    size = tile + width
    rows1 = width // 2
    rows2 = rows1 // cols
    rows3 = rows2 // depth if rows2 % (8 * depth) == 0 else rows2
    left, right = dft_halves(width)
    vmem = pl.BlockSpec(memory_space=pltpu.VMEM)
    hbm = pl.BlockSpec(memory_space=pltpu.HBM)
    semaphores = copies_needed(rows, cols)
    extended = (2, size // LANES, size, LANES)
    freq = (count, 2, width, width)
    refined = pl.pallas_call(
        refine_kernel,
        out_shape=(
            jax.ShapeDtypeStruct((2, tile, tile), F32),
            jax.ShapeDtypeStruct(coeffs.shape, F32),
        ),
        in_specs=[hbm] * 4 + [pl.BlockSpec(memory_space=pltpu.SMEM)] + [hbm] * 2,
        out_specs=(vmem, vmem),
        scratch_shapes=[
            pltpu.VMEM(extended, F32),
            pltpu.VMEM((2,) + extended, F32),
            pltpu.VMEM(extended, F32),
            pltpu.VMEM((count, 2, 5, 3 * width, LANES), F32),
            pltpu.VMEM(freq, F32),
            pltpu.VMEM(freq, F32),
            pltpu.VMEM(freq, BF16),
            pltpu.VMEM(freq, BF16),
            pltpu.VMEM((2, width, width), F32),
            pltpu.VMEM((2, 3, width, LANES), F32),
            pltpu.VMEM((count, width, width), F32),
            pltpu.VMEM(left.shape, BF16),
            pltpu.VMEM(right.shape, BF16),
            pltpu.VMEM((2, 2, 6, width, LANES), F32),
            pltpu.VMEM((2, 2, 6, rows1, LANES), F32),
            pltpu.VMEM((2, 2, cols - 1, 6, rows2, LANES), F32),
            pltpu.VMEM((2, 2, 6, rows2, LANES), F32),
            pltpu.VMEM((2, 2, depth - 1, 6, rows3, LANES), F32),
            pltpu.VMEM((2, 2, 3, width, LANES), F32),
            pltpu.VMEM((2, 2, 2, size // LANES, half, LANES), F32),
            pltpu.VMEM((2, 2, 2, half, LANES), F32),
            pltpu.VMEM((2, 2, 2, half, LANES), F32),
            pltpu.VMEM((4, half // 2, LANES), F32),
            pltpu.VMEM((4, half, LANES), F32),
            pltpu.VMEM((2, 2, half, LANES), F32),
            pltpu.VMEM((2, 2, half, LANES), F32),
            pltpu.VMEM((4, half // 2, LANES), F32),
            pltpu.VMEM((2, 2, tile, LANES), F32),
            pltpu.VMEM((2, 2, tile, LANES), F32),
            pltpu.VMEM((2, 8, LANES), F32),
            pltpu.VMEM((2, 8, LANES), F32),
            pltpu.VMEM((2, 8, LANES), F32),
            pltpu.VMEM((2, depth * cols - 1, 8, LANES), F32),
            pltpu.VMEM((3, width // LANES, width, LANES), F32),
            pltpu.VMEM((3, width, width), F32),
            pltpu.SemaphoreType.DMA((8,)),
            pltpu.SemaphoreType.DMA((semaphores,)),
            pltpu.SemaphoreType.DMA((semaphores,)),
        ],
        compiler_params=pltpu.CompilerParams(
            collective_id=0, has_side_effects=True, vmem_limit_bytes=60 * 1024 * 1024
        ),
        name="refine",
    )(object_field, probe, coeffs, patterns, jnp.swapaxes(offsets, 2, 3), left, right)
    return close(*refined)


def close_kernel(field, coeffs, field_out, coeffs_out, held, sems):
    planes = [(field.at[i], field_out.at[i]) for i in range(field.shape[0])]
    planes += [(coeffs.at[i], coeffs_out.at[i]) for i in range(coeffs.shape[0])]
    copies = [
        (pltpu.make_async_copy(source, held.at[n], sems.at[0, n]), pltpu.make_async_copy(held.at[n], target, sems.at[1, n]))
        for n, (source, target) in enumerate(planes)
    ]
    for come, _ in copies:
        come.start()
    for come, go in copies:
        come.wait()
        go.start()
    for _, go in copies:
        go.wait()


def close(field, coeffs):
    hbm = pl.BlockSpec(memory_space=pl.ANY)
    count = field.shape[0] + coeffs.shape[0]
    return pl.pallas_call(
        close_kernel,
        out_shape=tuple(jax.ShapeDtypeStruct(a.shape, a.dtype) for a in (field, coeffs)),
        in_specs=[hbm] * 2,
        out_specs=(hbm, hbm),
        scratch_shapes=[pltpu.VMEM((count,) + field.shape[1:], F32), pltpu.SemaphoreType.DMA((2, count))],
        compiler_params=pltpu.CompilerParams(vmem_limit_bytes=60 * 1024 * 1024),
        name="close",
    )(field, coeffs)


def solution(mesh):
    placed = (
        P(None, "row", "col"),
        P(),
        P(),
        P("row", "col", None, None, None),
        P("row", "col", None, None),
    )
    return jax.shard_map(
        local, mesh=mesh, in_specs=placed, out_specs=(P(None, "row", "col"), P()), check_vma=False
    )
```
